32 devices in a mesh: grp: 2 (over x), dp: 4 (over y, core), tp: 4 (over z).
Axes of the slice: x: 2, y: 2, z: 4, core: 2. Of those that a mesh axis runs over, the one named last changes fastest.
Arguments:
- query: bfloat16 [256, 6144], P(('grp', 'dp'), 'tp'), parts along dimension 0, may hold values from -200 to 200
- key_value_new: bfloat16 [256, 2048], P(('grp', 'dp'), 'tp'), parts along dimension 0, may hold values from -6 to 6
- key_value_cache: bfloat16 [256, 160, 2048], P(('grp', 'dp'), None, 'tp'), parts along dimension 0, may hold values from -7 to 7
- cache_len: int32 [256], P(('grp', 'dp')), parts along dimension 0, may hold values from 2 to 160, as said below
- out_proj: bfloat16 [6144, 6144], P('tp', 'dp'), may hold values from -0.078125 to 0.078125
- residual: bfloat16 [256, 6144], P('grp', 'dp'), parts along dimension 0, may hold values from -80 to 80
- norm_gain: float32 [6144], P('dp'), may hold values from 0.5 to 1.5
- routes: int32 [256, 2], P('grp'), parts along dimension 0, may hold values from 0 to 3, all different within a row; in each aligned block of 128 rows (0 to 127, 128 to 255, ...) at most 96 rows name the same one
- route_weight: float32 [256, 2], P('grp'), parts along dimension 0, may hold values from 0.25 to 1
- w_gate: bfloat16 [6144, 32768], P(None, ('dp', 'tp')), may hold values from -0.078125 to 0.078125
- w_up: bfloat16 [6144, 32768], P(None, ('dp', 'tp')), may hold values from -0.078125 to 0.078125
- w_down: bfloat16 [32768, 6144], P(('dp', 'tp')), may hold values from -0.09375 to 0.09375
Outputs:
- attended: bfloat16 [256, 6144], P(('grp', 'tp'), 'dp'), parts along dimension 0
- expert_mix: bfloat16 [256, 6144], P(('grp', 'tp'), 'dp'), parts along dimension 0
The draws below stay inside these ranges and needn't reach their ends.
There are 2 independent parts, one for each index of `grp`. The reference program is written for one: setup_inputs(seed, part) draws one part's arguments, and reference() takes and returns one part's arrays. A program takes and returns all parts, laid end to end along the dimension named above; an argument that names none is the same for every part. Nothing has to cross between parts.
Inputs may be any that keep to these rules, and one draw needn't show every extreme that they name: `cache_len`: in every block of 32 requests of one index of dp, one request has exactly 160. `routes`: each request names 2 different experts; no expert is named by more than 96 requests, a bound that some block reaches.
All inputs are finite; a program needn't handle non-finite values.
Results may differ from the reference program's by a relative error of at most 0.017.
Values may be sent and summed in bfloat16 or wider, within the bound.
No kernel may reach another device: no remote copies, remote signals or barrier semaphores. Data moves between devices by JAX's collectives and lax.ppermute only.
A program may use at most 256 MiB of HBM per device.

```python
import math
import jax
import jax.numpy as jnp
import numpy as np
from jax import lax

D = 6144
QUERY_HEADS = 48
KEY_VALUE_HEADS = 8
HEAD_SIZE = 128
EXPERTS = 4
FF = 8192
TOP = 2
ROWS_DEV = 32
CONTEXT_SLOTS = 160
REQUEST_ROWS = 128
CAP = 96


def shared_keys(key):
    first_part = jax.random.fold_in(key, 0)
    cache_tensor = jnp.clip(jax.random.normal(first_part, (REQUEST_ROWS, CONTEXT_SLOTS, KEY_VALUE_HEADS, 2, HEAD_SIZE), jnp.float32), -6.0, 6.0)
    blended = cache_tensor[:, 1, :, 0, :]
    return cache_tensor.at[:, 1, :, 0, :].set(blended)


def draw_key_value_cache(key, part):
    cache_tensor = shared_keys(key)
    return cache_tensor.reshape(REQUEST_ROWS, CONTEXT_SLOTS, KEY_VALUE_HEADS * 2 * HEAD_SIZE).astype(jnp.bfloat16)


def draw_query(key, part):
    key = jax.random.fold_in(key, 22)
    first_part = jax.random.fold_in(key, 0)
    value_rows = jnp.clip(jax.random.normal(first_part, (REQUEST_ROWS, KEY_VALUE_HEADS, QUERY_HEADS // KEY_VALUE_HEADS, HEAD_SIZE), jnp.float32), -6.0, 6.0)
    return value_rows.reshape(REQUEST_ROWS, QUERY_HEADS * HEAD_SIZE).astype(jnp.bfloat16)


def draw_cache_len(key, part):
    key = jax.random.fold_in(key, 5)
    first_part, second_part = jax.random.split(key)
    blocks = REQUEST_ROWS // ROWS_DEV
    base = jax.random.randint(first_part, (blocks, ROWS_DEV), 2, CONTEXT_SLOTS + 1, jnp.int32)
    pick = jax.random.randint(second_part, (blocks, 1), 0, ROWS_DEV, jnp.int32)
    where_full = jnp.arange(ROWS_DEV, dtype=jnp.int32)[None, :] == pick
    return jnp.where(where_full, CONTEXT_SLOTS, base).reshape(REQUEST_ROWS).astype(jnp.int32)


def draw_residual(key, part):
    key = jax.random.fold_in(key, 11)
    first_part = jax.random.fold_in(key, 0)
    base = jnp.clip(jax.random.normal(first_part, (REQUEST_ROWS, D), jnp.float32), -6.0, 6.0)
    column = jnp.arange(D, dtype=jnp.float32)[None, :] / D
    value_rows = base * 3.0 ** (column - 0.5)
    return value_rows.astype(jnp.bfloat16)


def raised(array, own_key, source, target, parts, factor):
    def block_of(dim):
        return (jnp.arange(array.shape[dim]) // (array.shape[dim] // parts)).reshape((-1,) + (1,) * (array.ndim - 1 - dim))

    one_side = jax.random.permutation(own_key, parts)[block_of(target)]
    far = (block_of(target) + parts // 2) % parts
    return jnp.where((block_of(source) == one_side) | (block_of(source) == far), factor * array, array)


def block_levels(key, dims, cuts, least, top_value):
    level = 1.0
    for dim, blocks in cuts:
        steps = jax.random.uniform(jax.random.fold_in(jax.random.fold_in(key, 6), dim), (blocks,), jnp.float32, least / len(cuts), top_value / len(cuts))
        level = level * jnp.repeat(jnp.exp(steps), dims[dim] // blocks).reshape((-1,) + (1,) * (len(dims) - 1 - dim))
    return level


def shared_out(key, own, number, rows, count, top, most, lean):
    order = jax.random.permutation(key, count)
    crowded, usual = load_shares(count, rows * top, most, lean, True), load_shares(count, rows * top, most, lean, False)
    places = jnp.arange(count)

    def named(tallies, rotation):
        used = int((tallies > 0).sum())
        fixed = max(1, used // 4)
        passed = fixed + (places - fixed + rotation * (used - fixed)) % max(1, count - fixed)
        return jnp.zeros((count,), jnp.int32).at[order[jnp.where(places < fixed, places, passed)]].set(jnp.asarray(tallies, jnp.int32))

    tallies = jnp.where(number % 4 == 0, named(crowded, number // 4), named(usual, number - number // 4 - 1))
    mixed = jax.random.permutation(jax.random.fold_in(own, 3), count)
    giver, taker = mixed[0:count // 2 * 2:2], mixed[1:count // 2 * 2:2]
    room = jnp.minimum(tallies[giver] - 1, most - tallies[taker]) // 2
    room = jnp.where((giver == order[0]) | (taker == order[0]) | (tallies[taker] == 0), 0, jnp.maximum(room, 0))
    passed = jax.random.randint(jax.random.fold_in(own, 4), (count // 2,), 0, 1 << 20) % (room + 1)
    tallies = tallies.at[giver].add(-passed).at[taker].add(passed)
    members = jnp.searchsorted(jnp.cumsum(tallies), jnp.arange(rows * top), side="right").astype(jnp.int32)
    table = members.reshape(top, rows).T
    table = table[jax.random.permutation(jax.random.fold_in(own, 1), rows)]
    rotation = jax.random.randint(jax.random.fold_in(own, 2), (rows, 1), 0, top)
    return jnp.take_along_axis(table, (jnp.arange(top)[None, :] + rotation) % top, axis=1)


def load_shares(number_of, total, limit, skew, full):
    weights = [(1 << 20) // math.isqrt(grade ** skew) + 1 for grade in range(1, number_of + 1)]
    largest = limit if full else min(limit, max(-(-total // number_of), total * weights[0] // sum(weights)))
    least = 1 if total - largest >= number_of - 1 else 0
    counts, spare = [largest] + [least] * (number_of - 1), total - largest - least * (number_of - 1)
    while spare > 0:
        free = [i for i in range(1, number_of) if counts[i] < largest] or [i for i in range(1, number_of) if counts[i] < limit]
        pool, budget = sum([weights[i] for i in free]), spare
        for i in free:
            extra = min(limit - counts[i], max(1, budget * weights[i] // pool), spare)
            counts[i] = counts[i] + extra
            spare = spare - extra
    return np.array(counts)


def gaussian(own_key, extent, deviation, most, shards=(), kind=jnp.bfloat16):
    level = block_levels(own_key, extent, shards, -0.22, 0.18) if shards else 1.0
    array = jax.random.normal(own_key, extent, jnp.float32) * deviation * level
    return jnp.minimum(jnp.maximum(array, -most), most).astype(kind)


def bell_draw_with(rng, dims, scale, reach, cuts, heavy, kind=jnp.bfloat16):
    entries = scale * jax.random.normal(rng, dims, jnp.float32)
    if cuts:
        entries = entries * block_levels(rng, dims, cuts, -0.22, 0.18)
    return jnp.clip(raised(entries, jax.random.fold_in(rng, 3), *heavy), -reach, reach).astype(kind)


def setup_inputs(seed: int = 0, part: int = 0) -> dict:
    streams_of = jax.random.split(jax.random.key(seed), 13)
    own_keys = jax.random.split(jax.random.fold_in(streams_of[12], part), 13)
    query = draw_query(jax.random.fold_in(jax.random.fold_in(streams_of[12], part), 71), part)
    key_value_new = gaussian(own_keys[1], (REQUEST_ROWS, KEY_VALUE_HEADS * 2 * HEAD_SIZE), 1.0, 6.0, ((0, 4), (1, 4)))
    key_value_cache = draw_key_value_cache(jax.random.fold_in(jax.random.fold_in(streams_of[12], part), 71), part)
    cache_len = draw_cache_len(jax.random.fold_in(jax.random.fold_in(streams_of[12], part), 71), part)
    out_proj = gaussian(streams_of[4], (QUERY_HEADS * HEAD_SIZE, D), (QUERY_HEADS * HEAD_SIZE) ** -0.5, 0.078125, ((0, 4), (1, 4)))
    residual = draw_residual(jax.random.fold_in(jax.random.fold_in(streams_of[12], part), 71), part)
    norm_gain = jnp.clip(1.0 + 0.1 * jax.random.normal(streams_of[6], (D,), jnp.float32), 0.5, 1.5)
    routes_keys = jax.random.split(jax.random.fold_in(own_keys[7], 1), REQUEST_ROWS // REQUEST_ROWS)
    routes_turns = jax.random.permutation(jax.random.fold_in(own_keys[7], 3), REQUEST_ROWS // REQUEST_ROWS)
    routes = jax.vmap(lambda own, number: shared_out(jax.random.fold_in(own_keys[7], 2), own, number, REQUEST_ROWS, EXPERTS, TOP, CAP, 2))(routes_keys, routes_turns).reshape((REQUEST_ROWS, TOP))
    route_weight = jnp.clip(jax.random.uniform(own_keys[8], (REQUEST_ROWS, TOP), jnp.float32, 0.25, 1.0), 0.25, 1.0)
    w_gate = gaussian(streams_of[9], (D, EXPERTS * FF), D ** -0.5, 0.078125, ((1, 16),))
    w_up = gaussian(streams_of[10], (D, EXPERTS * FF), D ** -0.5, 0.078125, ((1, 16),))
    w_down = bell_draw_with(streams_of[11], (EXPERTS * FF, D), FF ** -0.5, 0.09375, ((0, 16),), (0, 1, 16, 2.0))
    return dict(query=query, key_value_new=key_value_new, key_value_cache=key_value_cache, cache_len=cache_len, out_proj=out_proj, residual=residual, norm_gain=norm_gain, routes=routes, route_weight=route_weight, w_gate=w_gate, w_up=w_up, w_down=w_down)


EPS = 1e-05

def attend(query_heads, fresh_entry, cache_tensor, lengths):
    scale = 1.0 / HEAD_SIZE ** 0.5
    keys = cache_tensor[:, :, :, 0, :].astype(jnp.float32)
    value_rows = cache_tensor[:, :, :, 1, :].astype(jnp.float32)
    qf = query_heads.astype(jnp.float32)
    s_cache = jnp.einsum('rkgd,rckd->rkgc', qf, keys) * scale
    s_self = jnp.einsum('rkgd,rkd->rkg', qf, fresh_entry[:, :, 0, :].astype(jnp.float32)) * scale
    positions = jnp.arange(cache_tensor.shape[1], dtype=jnp.int32)
    valid = (positions[None, :] < lengths[:, None])[:, None, None, :]
    s_cache = jnp.where(valid, s_cache, -jnp.inf)
    top = jnp.maximum(lax.optimization_barrier(jnp.max(s_cache, axis=-1)), s_self)
    e_cache = jnp.where(valid, jnp.exp(s_cache - top[..., None]), 0.0)
    e_self = jnp.exp(s_self - top)
    total = lax.optimization_barrier(jnp.sum(e_cache, axis=-1)) + e_self
    p_cache = (e_cache / total[..., None]).astype(jnp.bfloat16)
    p_self = (e_self / total).astype(jnp.bfloat16)
    ctx = jnp.einsum('rkgc,rckd->rkgd', p_cache.astype(jnp.float32), value_rows)
    ctx = ctx + p_self.astype(jnp.float32)[..., None] * fresh_entry[:, :, None, 1, :].astype(jnp.float32)
    return ctx.astype(jnp.bfloat16).reshape(query_heads.shape[0], -1)

def make_slots(routes, experts, capacity):
    flat = routes.reshape(-1).astype(jnp.int32)
    count = flat.shape[0]
    onehot = (flat[:, None] == jnp.arange(experts, dtype=jnp.int32)[None, :]).astype(jnp.int32)
    rank = jnp.cumsum(onehot, axis=0) - onehot
    slot = lax.optimization_barrier(jnp.sum(rank * onehot, axis=1)).astype(jnp.int32)
    owner = (jnp.arange(count, dtype=jnp.int32) // routes.shape[1]).astype(jnp.int32)
    table = jnp.full((experts, capacity), routes.shape[0], jnp.int32).at[flat, slot].set(owner)
    return (flat, slot, table)

def expert_ffn(rows_in, wg, wu, wd):
    gate = jnp.dot(rows_in, wg, preferred_element_type=jnp.float32)
    up = jnp.dot(rows_in, wu, preferred_element_type=jnp.float32)
    hidden = (jax.nn.silu(gate) * up).astype(jnp.bfloat16)
    return jnp.dot(hidden, wd, preferred_element_type=jnp.float32)

def reference(query, key_value_new, key_value_cache, cache_len, out_proj, residual, norm_gain, routes, route_weight, w_gate, w_up, w_down):
    head_groups = QUERY_HEADS // KEY_VALUE_HEADS
    query_heads = query.reshape(REQUEST_ROWS, KEY_VALUE_HEADS, head_groups, HEAD_SIZE)
    fresh_entry = key_value_new.reshape(REQUEST_ROWS, KEY_VALUE_HEADS, 2, HEAD_SIZE)
    cache_tensor = key_value_cache.reshape(REQUEST_ROWS, CONTEXT_SLOTS, KEY_VALUE_HEADS, 2, HEAD_SIZE)
    context = attend(query_heads, fresh_entry, cache_tensor, cache_len)
    proj = jnp.dot(context, out_proj, preferred_element_type=jnp.float32)
    x = residual.astype(jnp.float32) + proj
    attended = x.astype(jnp.bfloat16)
    mean_sq = lax.optimization_barrier(jnp.mean(x * x, axis=1))
    normed = (x * lax.rsqrt(mean_sq + EPS)[:, None] * norm_gain[None, :]).astype(jnp.bfloat16)
    flat, slot, table = make_slots(routes, EXPERTS, CAP)
    outs = []
    for expert in range(EXPERTS):
        rows_in = jnp.take(normed, table[expert], axis=0, mode='fill', fill_value=0)
        lo = expert * FF
        outs.append(expert_ffn(rows_in, w_gate[:, lo:lo + FF], w_up[:, lo:lo + FF], w_down[lo:lo + FF, :]))
    per_expert = jnp.stack(outs)
    picked = per_expert[flat, slot]
    weighted = picked * route_weight.reshape(-1)[:, None]
    combined = lax.optimization_barrier(jnp.sum(weighted.reshape(REQUEST_ROWS, TOP, D), axis=1))
    return (attended, combined.astype(jnp.bfloat16))
```

```python
import functools

import jax
import jax.numpy as jnp
from jax import lax
from jax.experimental import pallas as pl
from jax.experimental.pallas import tpu as pltpu
from jax.sharding import PartitionSpec as P

QUERY_HEADS = 48
KEY_VALUE_HEADS = 8
HEAD_SIZE = 128
EXPERTS = 4
EPS = 1e-05
MIB = 1 << 20
VM = pltpu.VMEM
f32, bf16 = jnp.float32, jnp.bfloat16


def swap(x, axis, k):
    n = lax.axis_size(axis)
    return lax.ppermute(x, axis, [(i, i ^ k) for i in range(n)])


def whole(n):
    return [pl.BlockSpec(memory_space=VM) for _ in range(n)]


def attend_kernel(kv, group, len_ref, q_ref, new_ref, cache_ref, out_ref):
    batch, slots = cache_ref.shape[0], cache_ref.shape[1]
    first = pl.program_id(0) * batch
    scale = 1.0 / HEAD_SIZE**0.5
    pos = lax.broadcasted_iota(jnp.int32, (1, 8, slots), 2)
    valid = jnp.concatenate([pos < len_ref[first + b] for b in range(batch)], axis=0)
    for h in range(kv):
        lo = 2 * h * HEAD_SIZE
        q = q_ref[:, h]
        keys = cache_ref[:, :, lo : lo + HEAD_SIZE]
        vals = cache_ref[:, :, lo + HEAD_SIZE : lo + 2 * HEAD_SIZE]
        new_k = new_ref[:, :, lo : lo + HEAD_SIZE].astype(f32)
        new_v = new_ref[:, :, lo + HEAD_SIZE : lo + 2 * HEAD_SIZE].astype(f32)
        s = lax.dot_general(q, keys, (((2,), (2,)), ((0,), (0,))), preferred_element_type=f32)
        s = jnp.where(valid, s * scale, -jnp.inf)
        s_new = jnp.sum(q.astype(f32) * new_k, axis=2, keepdims=True) * scale
        top = jnp.maximum(jnp.max(s, axis=2, keepdims=True), s_new)
        e = jnp.exp(s - top)
        e_new = jnp.exp(s_new - top)
        inv = 1.0 / (jnp.sum(e, axis=2, keepdims=True) + e_new)
        p = (e * inv).astype(bf16)
        p_new = (e_new * inv).astype(bf16).astype(f32)
        ctx = lax.dot_general(p, vals, (((2,), (1,)), ((0,), (0,))), preferred_element_type=f32)
        ctx = ctx + p_new * new_v
        out_ref[:, h] = ctx.astype(bf16)


def attend(query, key_value_new, cache, cache_len):
    rows, slots, width = cache.shape
    kv = width // (2 * HEAD_SIZE)
    group = QUERY_HEADS // KEY_VALUE_HEADS
    q = query.reshape(rows, kv, group, HEAD_SIZE)
    q = jnp.pad(q, ((0, 0), (0, 0), (0, 8 - group), (0, 0)))
    new = key_value_new.reshape(rows, 1, width)
    batch = 8
    out = pl.pallas_call(
        functools.partial(attend_kernel, kv, group),
        out_shape=jax.ShapeDtypeStruct((rows, kv, 8, HEAD_SIZE), bf16),
        grid_spec=pltpu.PrefetchScalarGridSpec(
            num_scalar_prefetch=1,
            grid=(rows // batch,),
            in_specs=[
                pl.BlockSpec((batch, kv, 8, HEAD_SIZE), lambda i, n: (i, 0, 0, 0)),
                pl.BlockSpec((batch, 1, width), lambda i, n: (i, 0, 0)),
                pl.BlockSpec((batch, slots, width), lambda i, n: (i, 0, 0)),
            ],
            out_specs=pl.BlockSpec((batch, kv, 8, HEAD_SIZE), lambda i, n: (i, 0, 0, 0)),
        ),
        compiler_params=pltpu.CompilerParams(vmem_limit_bytes=24 * MIB),
        name="attention",
    )(cache_len, q, new, cache)
    return out[:, :, :group].reshape(rows, kv * group * HEAD_SIZE)


def project_kernel(n_dp, n_tp, place_ref, *refs):
    ctx = refs[:n_dp]
    w_ref, res_ref = refs[n_dp], refs[n_dp + 1]
    outs = refs[n_dp + 2 : n_dp + 2 + n_tp]
    held, prod = refs[n_dp + 2 + n_tp :]
    j, t = place_ref[0], place_ref[1]
    rows = ctx[0].shape[0]
    share = outs[0].shape[0]
    for k in range(n_dp):
        held[pl.ds(pl.multiple_of((j ^ k) * rows, rows), rows), :] = ctx[k][...]
    prod[...] = jnp.dot(held[...], w_ref[...], preferred_element_type=f32)
    mine = pl.ds(pl.multiple_of(t * share, share), share)
    outs[0][...] = prod[mine, :] + res_ref[mine, :].astype(f32)
    for k in range(1, n_tp):
        outs[k][...] = prod[pl.ds(pl.multiple_of((t ^ k) * share, share), share), :].astype(bf16)


def project(place, ctx, out_proj, residual, n_tp):
    n_dp = len(ctx)
    total, width = residual.shape
    share = total // n_tp
    depth = out_proj.shape[0]
    return pl.pallas_call(
        functools.partial(project_kernel, n_dp, n_tp),
        out_shape=[jax.ShapeDtypeStruct((share, width), f32 if k == 0 else bf16) for k in range(n_tp)],
        in_specs=[pl.BlockSpec(memory_space=pltpu.SMEM)] + whole(n_dp + 2),
        out_specs=whole(n_tp),
        scratch_shapes=[VM((total, depth), bf16), VM((total, width), f32)],
        compiler_params=pltpu.CompilerParams(vmem_limit_bytes=24 * MIB),
        name="projection",
    )(place, *ctx, out_proj, residual)


def chunk_of(width):
    return 512 if width % 512 == 0 else width


def gate_up_stream(j, ks, x_refs, g_refs, wg, wu, buf_g, buf_u, sem, add, after_start):
    depth, step = buf_g.shape[0], buf_g.shape[1]
    width = x_refs[0].shape[1]
    chunks = [(i, c) for i in range(len(ks)) for c in range(width // step)]

    def copies(n):
        i, c = chunks[n]
        slot = n % depth
        rows = pl.ds(pl.multiple_of((j ^ ks[i]) * width + c * step, 128), step)
        return (
            pltpu.make_async_copy(wg.at[rows, :], buf_g.at[slot], sem.at[0, slot]),
            pltpu.make_async_copy(wu.at[rows, :], buf_u.at[slot], sem.at[1, slot]),
        )

    for n in range(min(depth, len(chunks))):
        for c in copies(n):
            c.start()
    after_start()
    for n in range(len(chunks)):
        i, c = chunks[n]
        cols = slice(c * step, (c + 1) * step)
        x = x_refs[i][:, cols].astype(f32)
        xs = (x * g_refs[i][:, cols]).astype(bf16)
        sq = x * x
        part = sum(sq[:, l : l + 128] for l in range(0, step, 128))
        one, two = copies(n)
        slot = n % depth
        one.wait()
        g = jnp.dot(xs, buf_g[slot], preferred_element_type=f32)
        two.wait()
        u = jnp.dot(xs, buf_u[slot], preferred_element_type=f32)
        add(n == 0, g, u, part)
        if n + depth < len(chunks):
            for c in copies(n + depth):
                c.start()


def first_kernel(ks, place_ref, *refs):
    n = len(ks)
    x_refs, g_refs = refs[:n], refs[n : 2 * n]
    wg, wu, acc_g, acc_u, sq, buf_g, buf_u, sem = refs[2 * n :]

    def add(fresh, g, u, part):
        acc_g[...] = g if fresh else acc_g[...] + g
        acc_u[...] = u if fresh else acc_u[...] + u
        sq[...] = part if fresh else sq[...] + part

    gate_up_stream(place_ref[0], ks, x_refs, g_refs, wg, wu, buf_g, buf_u, sem, add, lambda: None)


def first_part(place, ks, xs, gains, w_gate, w_up):
    rows, width = xs[0].shape
    hidden = w_gate.shape[1]
    step = chunk_of(width)
    return pl.pallas_call(
        functools.partial(first_kernel, ks),
        out_shape=[
            jax.ShapeDtypeStruct((rows, hidden), f32),
            jax.ShapeDtypeStruct((rows, hidden), f32),
            jax.ShapeDtypeStruct((rows, 128), f32),
        ],
        in_specs=[pl.BlockSpec(memory_space=pltpu.SMEM)] + whole(2 * len(ks)) + [pl.BlockSpec(memory_space=pl.ANY)] * 2,
        out_specs=whole(3),
        scratch_shapes=[
            VM((3, step, hidden), bf16),
            VM((3, step, hidden), bf16),
            pltpu.SemaphoreType.DMA((2, 3)),
        ],
        compiler_params=pltpu.CompilerParams(vmem_limit_bytes=28 * MIB),
        name="gate_up_first",
    )(place, *xs, *gains, w_gate, w_up)


def down_copies(j, blocks, wd, buf, sem, width):
    step = buf.shape[2]
    depth = buf.shape[0]
    chunks = [(i, c) for i in range(len(blocks)) for c in range(width // step)]

    def copy(n):
        i, c = chunks[n]
        cols = pl.ds(pl.multiple_of((j ^ blocks[i]) * width + c * step, 128), step)
        return pltpu.make_async_copy(wd.at[:, cols], buf.at[n % depth], sem.at[n % depth])

    def start():
        for n in range(min(depth, len(chunks))):
            copy(n).start()

    def run(h, put):
        for n in range(len(chunks)):
            i, c = chunks[n]
            copy(n).wait()
            put(i, slice(c * step, (c + 1) * step), jnp.dot(h, buf[n % depth], preferred_element_type=f32))
            if n + depth < len(chunks):
                copy(n + depth).start()

    return start, run


def second_kernel(ks, blocks, model, place_ref, *refs):
    n, m = len(ks), len(blocks)
    x_refs, g_refs = refs[:n], refs[n : 2 * n]
    in_g, in_u, in_sq, weight, wg, wu, wd = refs[2 * n : 2 * n + 7]
    outs = refs[2 * n + 7 : 2 * n + 7 + m]
    h_ref, acc_g, acc_u, sq, buf_g, buf_u, buf_d, sem, sem_d = refs[2 * n + 7 + m :]
    j = place_ref[0]
    start, run = down_copies(j, blocks, wd, buf_d, sem_d, outs[0].shape[1])

    def add(fresh, g, u, part):
        acc_g[...] = (in_g if fresh else acc_g)[...] + g
        acc_u[...] = (in_u if fresh else acc_u)[...] + u
        sq[...] = (in_sq if fresh else sq)[...] + part

    gate_up_stream(j, ks, x_refs, g_refs, wg, wu, buf_g, buf_u, sem, add, start)
    scale = lax.rsqrt(jnp.sum(sq[...], axis=1, keepdims=True) / model + EPS)
    g = acc_g[...] * scale
    u = acc_u[...] * (scale * weight[...])
    h_ref[...] = (g / (1.0 + jnp.exp(-g)) * u).astype(bf16)

    def put(i, cols, value):
        outs[i][:, cols] = value.astype(bf16)

    run(h_ref[...], put)


def second_part(place, ks, blocks, xs, gains, acc_g, acc_u, sq, weight, w_gate, w_up, w_down):
    rows, width = xs[0].shape
    hidden = w_gate.shape[1]
    step = chunk_of(width)
    res = pl.pallas_call(
        functools.partial(second_kernel, ks, blocks, w_down.shape[1]),
        out_shape=[jax.ShapeDtypeStruct((rows, width), bf16) for _ in blocks]
        + [jax.ShapeDtypeStruct((rows, hidden), bf16)],
        in_specs=[pl.BlockSpec(memory_space=pltpu.SMEM)]
        + whole(2 * len(ks) + 4)
        + [pl.BlockSpec(memory_space=pl.ANY)] * 3,
        out_specs=whole(len(blocks) + 1),
        scratch_shapes=[
            VM((rows, hidden), f32),
            VM((rows, hidden), f32),
            VM((rows, 128), f32),
            VM((3, step, hidden), bf16),
            VM((3, step, hidden), bf16),
            VM((3, hidden, step), bf16),
            pltpu.SemaphoreType.DMA((2, 3)),
            pltpu.SemaphoreType.DMA((3,)),
        ],
        compiler_params=pltpu.CompilerParams(vmem_limit_bytes=44 * MIB),
        name="gate_up_second",
    )(place, *xs, *gains, acc_g, acc_u, sq, weight, w_gate, w_up, w_down)
    return res[:-1], res[-1]


def down_kernel(blocks, added, place_ref, h_ref, *refs):
    n_add = sum(added)
    adds = iter(refs[:n_add])
    adds = [next(adds) if a else None for a in added]
    wd = refs[n_add]
    outs = refs[n_add + 1 : n_add + 1 + len(blocks)]
    buf, sem = refs[n_add + 1 + len(blocks) :]
    start, run = down_copies(place_ref[0], blocks, wd, buf, sem, outs[0].shape[1])
    start()

    def put(i, cols, value):
        if adds[i] is not None:
            value = value + adds[i][:, cols].astype(f32)
        outs[i][:, cols] = value.astype(outs[i].dtype)

    run(h_ref[...], put)


def down_part(place, blocks, h, adds, types, w_down, width):
    rows, hidden = h.shape
    step = chunk_of(width)
    given = [a for a in adds if a is not None]
    return pl.pallas_call(
        functools.partial(down_kernel, blocks, [a is not None for a in adds]),
        out_shape=[jax.ShapeDtypeStruct((rows, width), t) for t in types],
        in_specs=[pl.BlockSpec(memory_space=pltpu.SMEM)] + whole(1 + len(given)) + [pl.BlockSpec(memory_space=pl.ANY)],
        out_specs=whole(len(blocks)),
        scratch_shapes=[VM((4, hidden, step), bf16), pltpu.SemaphoreType.DMA((4,))],
        compiler_params=pltpu.CompilerParams(vmem_limit_bytes=28 * MIB),
        name="down",
    )(place, h, *given, w_down)


def gather_dp(x):
    n = lax.axis_size("dp")
    far = {k: swap(x, "dp", k) for k in range(2, n, 2)}
    out = [None] * n
    out[0], out[1] = x, swap(x, "dp", 1)
    for k in range(2, n, 2):
        out[k] = far[k]
        out[k + 1] = swap(far[k], "dp", 1)
    return out


def body(
    query,
    key_value_new,
    key_value_cache,
    cache_len,
    out_proj,
    residual,
    norm_gain,
    routes,
    route_weight,
    w_gate,
    w_up,
    w_down,
):
    n_dp = lax.axis_size("dp")
    n_tp = lax.axis_size("tp")
    j, t = lax.axis_index("dp"), lax.axis_index("tp")
    place = jnp.stack([j, t]).astype(jnp.int32)
    total, width = residual.shape
    share = total // n_tp

    gains = gather_dp(norm_gain[None, :])
    expert = j // (n_dp // EXPERTS)
    weight = jnp.sum(jnp.where(routes == expert, route_weight, 0.0), axis=1, keepdims=True)

    context = attend(query, key_value_new, key_value_cache, cache_len)
    parts = project(place, gather_dp(context), out_proj, residual, n_tp)
    x = parts[0]
    for k in range(1, n_tp):
        x = x + swap(parts[k], "tp", k).astype(f32)
    attended = x.astype(bf16)

    others = [attended] + [swap(attended, "tp", k) for k in range(1, n_tp)]
    stacked = jnp.zeros((n_tp, share, width), bf16)
    for k in range(n_tp):
        stacked = lax.dynamic_update_slice(stacked, others[k][None], (t ^ k, 0, 0))
    mine = stacked.reshape(total, width)

    xs = gather_dp(mine)
    near, far = (0, 1), tuple(range(2, n_dp))
    acc_g, acc_u, sq = first_part(place, near, [xs[k] for k in near], [gains[k] for k in near], w_gate, w_up)
    odd = tuple(range(3, n_dp, 2))
    even = tuple(range(2, n_dp, 2))
    out_odd, h = second_part(
        place, far, odd, [xs[k] for k in far], [gains[k] for k in far], acc_g, acc_u, sq, weight, w_gate, w_up, w_down
    )
    crossed = [swap(o, "dp", 1) for o in out_odd]
    sums = down_part(place, even, h, crossed, [bf16] * len(even), w_down, width)
    arrived = [swap(s, "dp", k) for s, k in zip(sums, even)]
    near_out = down_part(place, (1, 0), h, [None, None], [bf16, f32], w_down, width)
    mix = near_out[1] + swap(near_out[0], "dp", 1).astype(f32)
    for a in arrived:
        mix = mix + a.astype(f32)
    blocks = mix.reshape(n_tp, share, width)
    result = lax.dynamic_index_in_dim(blocks, t, 0, keepdims=False)
    for k in range(1, n_tp):
        piece = lax.dynamic_index_in_dim(blocks, t ^ k, 0, keepdims=False).astype(bf16)
        result = result + swap(piece, "tp", k).astype(f32)
    return (attended, result.astype(bf16))


def solution(mesh):
    in_specs = (
        P(("grp", "dp"), "tp"),
        P(("grp", "dp"), "tp"),
        P(("grp", "dp"), None, "tp"),
        P(("grp", "dp")),
        P("tp", "dp"),
        P("grp", "dp"),
        P("dp"),
        P("grp", None),
        P("grp", None),
        P(None, ("dp", "tp")),
        P(None, ("dp", "tp")),
        P(("dp", "tp"), None),
    )
    out_specs = (P(("grp", "tp"), "dp"), P(("grp", "tp"), "dp"))
    return jax.shard_map(body, mesh=mesh, in_specs=in_specs, out_specs=out_specs, check_vma=False)
```

```python
import functools

import jax
import jax.numpy as jnp
from jax import lax
from jax.experimental import pallas as pl
from jax.experimental.pallas import tpu as pltpu
from jax.sharding import PartitionSpec as P

QUERY_HEADS = 48
KEY_VALUE_HEADS = 8
HEAD_SIZE = 128
EXPERTS = 4
EPS = 1e-05
TAIL = 128
MIB = 1 << 20
VM = pltpu.VMEM
f32, bf16 = jnp.float32, jnp.bfloat16
SMEM_SPEC = pl.BlockSpec(memory_space=pltpu.SMEM)
HBM_SPEC = pl.BlockSpec(memory_space=pltpu.HBM)
VMEM_SPEC = pl.BlockSpec(memory_space=VM)


def swap(x, axis, k):
    n = lax.axis_size(axis)
    return lax.ppermute(x, axis, [(i, i ^ k) for i in range(n)])


def hbm(x):
    return pltpu.with_memory_space_constraint(x, pltpu.HBM)


def cost(nbytes, flops=0):
    return pl.CostEstimate(flops=int(flops), bytes_accessed=int(nbytes), transcendentals=0)


def row_loads(place_ref, mats, ks, outs, sem):
    loads = []
    for i, k in enumerate(ks):
        width = outs[i].shape[0]
        rows = pl.ds(pl.multiple_of((place_ref[0] ^ k) * width, 128), width)
        loads.append(pltpu.make_async_copy(mats[i].at[rows, :], outs[i], sem.at[i]))
    return loads


def col_loads(place_ref, mat, ks, outs, sem):
    loads = []
    for i, k in enumerate(ks):
        width = outs[i].shape[1]
        cols = pl.ds(pl.multiple_of((place_ref[0] ^ k) * width, 128), width)
        loads.append(pltpu.make_async_copy(mat.at[:, cols], outs[i], sem.at[i]))
    return loads


def all_of(loads, act):
    for c in loads:
        getattr(c, act)()


def attend_kernel(kv, group, batch, _, len_hbm, q_hbm, new_hbm, cache_hbm, w_hbm, *refs):
    out_ref, w_ref, len_ref, q_ref, new_ref, cache, q_scr, sem, w_sem, small_sem = refs
    rows, slots = cache.shape[0], cache.shape[1]
    small = [
        pltpu.make_async_copy(a, b, small_sem.at[i])
        for i, (a, b) in enumerate(((q_hbm, q_ref), (new_hbm, new_ref), (len_hbm, len_ref)))
    ]
    all_of(small, "start")
    parts = [pl.ds(i * batch, batch) for i in range(rows // batch)]
    loads = [pltpu.make_async_copy(cache_hbm.at[p], cache.at[p], sem.at[i]) for i, p in enumerate(parts)]
    all_of(loads, "start")
    after = pltpu.make_async_copy(w_hbm, w_ref, w_sem)
    after.start()
    all_of(small, "wait")
    scale = 1.0 / HEAD_SIZE**0.5
    q_scr[...] = jnp.zeros_like(q_scr)
    for h in range(kv):
        for g in range(group):
            lo = (h * group + g) * HEAD_SIZE
            q_scr[h, :, g, :] = q_ref[:, lo : lo + HEAD_SIZE].astype(f32)
    pos = lax.broadcasted_iota(jnp.int32, (1, 8, slots), 2)
    new = new_ref[...].astype(f32)
    for i, p in enumerate(parts):
        base = i * batch
        valid = jnp.concatenate([pos < len_ref[base + b] for b in range(batch)], axis=0)
        loads[i].wait()
        for h in range(kv):
            lo = 2 * h * HEAD_SIZE

            def spread(col):
                return jnp.concatenate(
                    [
                        jnp.broadcast_to(new[base + b : base + b + 1, col : col + HEAD_SIZE][None], (1, 8, HEAD_SIZE))
                        for b in range(batch)
                    ],
                    axis=0,
                )

            q = q_scr[h, p]
            keys = cache[p, :, lo : lo + HEAD_SIZE]
            vals = cache[p, :, lo + HEAD_SIZE : lo + 2 * HEAD_SIZE]
            s = lax.dot_general(
                q.astype(bf16), keys, (((2,), (2,)), ((0,), (0,))), preferred_element_type=f32
            )
            s = jnp.where(valid, s * scale, -jnp.inf)
            s_new = jnp.sum(q * spread(lo), axis=2, keepdims=True) * scale
            top = jnp.maximum(jnp.max(s, axis=2, keepdims=True), s_new)
            e = jnp.exp(s - top)
            e_new = jnp.exp(s_new - top)
            inv = 1.0 / (jnp.sum(e, axis=2, keepdims=True) + e_new)
            probs = (e * inv).astype(bf16)
            p_new = (e_new * inv).astype(bf16).astype(f32)
            ctx = lax.dot_general(probs, vals, (((2,), (1,)), ((0,), (0,))), preferred_element_type=f32)
            q_scr[h, p] = ctx + p_new * spread(lo + HEAD_SIZE)
    for h in range(kv):
        for g in range(group):
            lo = (h * group + g) * HEAD_SIZE
            out_ref[:, lo : lo + HEAD_SIZE] = q_scr[h, :, g, :].astype(bf16)
    after.wait()


def attend(place, query, key_value_new, cache, cache_len, out_proj):
    rows, slots, width = cache.shape
    kv = width // (2 * HEAD_SIZE)
    group = QUERY_HEADS // KEY_VALUE_HEADS
    batch = 8
    return pl.pallas_call(
        functools.partial(attend_kernel, kv, group, batch),
        out_shape=[jax.ShapeDtypeStruct(query.shape, bf16), VM(out_proj.shape, bf16)],
        in_specs=[SMEM_SPEC] + [HBM_SPEC] * 5,
        out_specs=[VMEM_SPEC] * 2,
        scratch_shapes=[
            pltpu.SMEM(cache_len.shape, jnp.int32),
            VM(query.shape, bf16),
            VM(key_value_new.shape, bf16),
            VM(cache.shape, bf16),
            VM((kv, rows, 8, HEAD_SIZE), f32),
            pltpu.SemaphoreType.DMA((rows // batch,)),
            pltpu.SemaphoreType.DMA,
            pltpu.SemaphoreType.DMA((3,)),
        ],
        compiler_params=pltpu.CompilerParams(vmem_limit_bytes=10 * MIB),
        cost_estimate=cost(4 * cache.size, 24 * cache.size),
        name="attention",
    )(place, *[hbm(a) for a in (cache_len, query, key_value_new, cache, out_proj)])


def fetch_kernel(ks, place_ref, token_ref, *refs):
    n = len(ks)
    mats, outs, token_out, sem = refs[:n], refs[n : 2 * n], refs[2 * n], refs[2 * n + 1]
    loads = row_loads(place_ref, mats, ks, outs, sem)
    all_of(loads, "start")
    token_out[...] = token_ref[:8, :128]
    all_of(loads, "wait")


def fetch(place, token, wanted, width):
    ks = [k for _, k in wanted]
    n = len(wanted)
    res = pl.pallas_call(
        functools.partial(fetch_kernel, ks),
        out_shape=[VM((width, m.shape[1]), bf16) for m, _ in wanted] + [jax.ShapeDtypeStruct((8, 128), token.dtype)],
        in_specs=[SMEM_SPEC, VMEM_SPEC] + [HBM_SPEC] * n,
        out_specs=[VMEM_SPEC] * (n + 1),
        scratch_shapes=[pltpu.SemaphoreType.DMA((n,))],
        compiler_params=pltpu.CompilerParams(vmem_limit_bytes=MIB),
        cost_estimate=cost(sum(2 * width * m.shape[1] for m, _ in wanted)),
        name="fetch",
    )(place, token, *[hbm(m) for m, _ in wanted])
    return res[:n], res[n]


def project_kernel(keep, sent, place_ref, *refs):
    n_dp = len(refs) - 5
    ctx, w_ref, keep_ref, send_ref, held, prod = refs[:n_dp], *refs[n_dp:]
    j, t = place_ref[0], place_ref[1]
    rows = ctx[0].shape[0]
    share = keep_ref.shape[0] // len(keep)
    for k in range(n_dp):
        held[pl.ds(pl.multiple_of((j ^ k) * rows, rows), rows), :] = ctx[k][...]
    prod[...] = jnp.dot(held[...], w_ref[...], preferred_element_type=f32)
    for i, k in enumerate(sent):
        block = pl.ds(pl.multiple_of((t ^ k) * share, share), share)
        send_ref[i * share : (i + 1) * share, :] = prod[block, :].astype(bf16)
    for i, k in enumerate(keep):
        block = pl.ds(pl.multiple_of((t ^ k) * share, share), share)
        keep_ref[i * share : (i + 1) * share, :] = prod[block, :]


def project(place, ctx, out_proj, total, keep, sent):
    width = out_proj.shape[1]
    share = total // (len(keep) + len(sent))
    depth = out_proj.shape[0]
    return pl.pallas_call(
        functools.partial(project_kernel, keep, sent),
        out_shape=[
            jax.ShapeDtypeStruct((len(keep) * share, width), f32),
            jax.ShapeDtypeStruct((len(sent) * share, width), bf16),
        ],
        in_specs=[SMEM_SPEC] + [VMEM_SPEC] * (len(ctx) + 1),
        out_specs=[VMEM_SPEC] * 2,
        scratch_shapes=[VM((total, depth), bf16), VM((total, width), f32)],
        compiler_params=pltpu.CompilerParams(vmem_limit_bytes=4 * MIB),
        cost_estimate=cost(2 * out_proj.size, 2 * total * out_proj.size),
        name="projection",
    )(place, *ctx, out_proj)


def sum_kernel(own_ref, got_ref, token_ref, sum_ref, pass_ref):
    total = own_ref[...] + got_ref[...].astype(f32)
    sum_ref[...] = total
    pass_ref[...] = total.astype(bf16)


def pass_kernel(x_ref, token_ref, out_ref):
    out_ref[...] = x_ref[...]


def passed_on(x, token):
    return pl.pallas_call(
        pass_kernel,
        out_shape=jax.ShapeDtypeStruct(x.shape, x.dtype),
        in_specs=[VMEM_SPEC] * 2,
        out_specs=VMEM_SPEC,
        compiler_params=pltpu.CompilerParams(vmem_limit_bytes=2 * MIB),
        name="passed_on",
    )(x, token)


def add_up(own, got, token):
    return pl.pallas_call(
        sum_kernel,
        out_shape=[jax.ShapeDtypeStruct(own.shape, f32), jax.ShapeDtypeStruct(own.shape, bf16)],
        in_specs=[VMEM_SPEC] * 3,
        out_specs=[VMEM_SPEC] * 2,
        compiler_params=pltpu.CompilerParams(vmem_limit_bytes=4 * MIB),
        name="pair_sum",
    )(own, got, token)


def stream_kernel(keep, arrived, place_ref, sum_ref, *refs):
    n = len(arrived)
    got, (res_ref, gain_ref, _, att_ref, msg_ref) = refs[:n], refs[n:]
    share, width = att_ref.shape
    t = place_ref[1]
    for i, k in enumerate(keep):
        x = sum_ref[i * share : (i + 1) * share, :]
        for a, m in enumerate(arrived):
            place = keep.index(k ^ m)
            x = x + got[a][place * share : (place + 1) * share, :].astype(f32)
        x = x + res_ref[pl.ds(pl.multiple_of((t ^ k) * share, share), share), :].astype(f32)
        if i == 0:
            att_ref[...] = x.astype(bf16)
        rows = slice(i * share, (i + 1) * share)
        msg_ref[rows, :width] = (x * gain_ref[...][None, :]).astype(bf16)
        left = jnp.sum(x * x, axis=1, keepdims=True)
        lane = lax.broadcasted_iota(jnp.int32, (share, TAIL), 1)
        tail = jnp.zeros((share, TAIL), f32)
        for piece in range(3):
            high = left.astype(bf16).astype(f32)
            tail = jnp.where(lane == piece, high, tail)
            left = left - high
        msg_ref[rows, width:] = tail.astype(bf16)


def stream(place, total, got, arrived, residual, gain, token, keep):
    rows, width = total.shape
    share = rows // len(keep)
    return pl.pallas_call(
        functools.partial(stream_kernel, keep, arrived),
        out_shape=[VM((share, width), bf16), jax.ShapeDtypeStruct((rows, width + TAIL), bf16)],
        in_specs=[SMEM_SPEC] + [VMEM_SPEC] * (len(got) + 4),
        out_specs=[VMEM_SPEC] * 2,
        compiler_params=pltpu.CompilerParams(vmem_limit_bytes=4 * MIB),
        name="residual_stream",
    )(place, total, *got, residual, gain, token)


def weights_kernel(owners, order, place_ref, routes_ref, given_ref, token_ref, out_ref):
    j, t = place_ref[0], place_ref[1]
    total = out_ref.shape[0]
    share = total // len(order)
    mine = jnp.where(routes_ref[...] == j // owners, given_ref[...], 0.0)
    mine = jnp.sum(mine, axis=0, keepdims=True)
    lane = lax.broadcasted_iota(jnp.int32, (share, total), 1)
    row = lax.broadcasted_iota(jnp.int32, (share, total), 0)
    for i, k in enumerate(order):
        picked = jnp.where(lane == (t ^ k) * share + row, mine, 0.0)
        out_ref[i * share : (i + 1) * share, :] = jnp.sum(picked, axis=1, keepdims=True)


def request_weights(place, routes, given, token, owners, order):
    return pl.pallas_call(
        functools.partial(weights_kernel, owners, order),
        out_shape=jax.ShapeDtypeStruct((routes.shape[1], 1), f32),
        in_specs=[SMEM_SPEC] + [VMEM_SPEC] * 3,
        out_specs=VMEM_SPEC,
        compiler_params=pltpu.CompilerParams(vmem_limit_bytes=4 * MIB),
        name="request_weights",
    )(place, routes, given, token)


def join(x_ref, parts, width):
    at = 0
    sq = []
    for p in parts:
        n = p.shape[0]
        x_ref[at : at + n, :] = p[:, :width]
        sq.append(jnp.sum(p[:, width:].astype(f32), axis=1, keepdims=True))
        at += n
    return jnp.concatenate(sq, axis=0)


def grow_kernel(first, odd, model, row_ks, ks, place_ref, *refs):
    last = odd is not None
    (a_ref, b_ref, gate, up), refs = refs[:4], refs[4:]
    if not first:
        (in_g, in_u, in_sq), refs = refs[:3], refs[3:]
    if last:
        weight, ready, refs = refs[0], refs[1 : 1 + len(odd)], refs[1 + len(odd) :]
    n = len(row_ks)
    mats, wd, refs = refs[:n], refs[n], refs[n + 1 :]
    if last:
        outs, h_ref, refs = refs[: len(odd)], refs[len(odd)], refs[len(odd) + 1 :]
    else:
        (acc_g, acc_u, sq_ref), refs = refs[:3], refs[3:]
    rows_loaded, loaded, (x_ref, row_sem, sem) = refs[:n], refs[n : n + len(ks)], refs[n + len(ks) :]
    loads = row_loads(place_ref, mats, row_ks, rows_loaded, row_sem) + col_loads(place_ref, wd, ks, loaded, sem)
    all_of(loads, "start")
    sq = join(x_ref, (a_ref, b_ref), x_ref.shape[1])
    if not first:
        sq = sq + in_sq[...]

    def columns(cols):
        g = jnp.dot(x_ref[...], gate[:, cols], preferred_element_type=f32)
        u = jnp.dot(x_ref[...], up[:, cols], preferred_element_type=f32)
        if not first:
            g, u = g + in_g[:, cols], u + in_u[:, cols]
        if last:
            scale = lax.rsqrt(sq / model + EPS)
            g, u = g * scale, u * (scale * weight[...])
            h_ref[:, cols] = (g / (1.0 + jnp.exp(-g)) * u).astype(bf16)
        else:
            acc_g[:, cols], acc_u[:, cols] = g, u

    hidden = gate.shape[1]
    if loads:

        @pl.loop(0, 2)
        def _(c):
            columns(pl.ds(pl.multiple_of(c * (hidden // 2), 128), hidden // 2))
    else:
        step = min(512, hidden)
        for lo in range(0, hidden, step):
            columns(slice(lo, lo + step))
    if last:
        for i in range(len(odd)):
            outs[i][...] = jnp.dot(h_ref[...], ready[i][...], preferred_element_type=f32).astype(bf16)
    else:
        sq_ref[...] = sq
    all_of(loads, "wait")


def grow(place, parts, gate, up, acc, ahead, down, ks, model, last):
    rows = parts[0].shape[0] + parts[1].shape[0]
    width, hidden = gate.shape
    args = [*parts, gate, up] + (list(acc) if acc is not None else [])
    odd = None
    if last is not None:
        weight, odd, ready = last
        args += [weight, *ready]
        outs = [jax.ShapeDtypeStruct((rows, width), bf16) for _ in odd] + [jax.ShapeDtypeStruct((rows, hidden), bf16)]
    else:
        outs = [jax.ShapeDtypeStruct((rows, n), f32) for n in (hidden, hidden, 1)]
    own = len(outs)
    res = pl.pallas_call(
        functools.partial(grow_kernel, acc is None, odd, model, [k for _, k in ahead], ks),
        out_shape=outs + [VM((width, hidden), bf16) for _ in ahead] + [VM((hidden, width), bf16) for _ in ks],
        in_specs=[SMEM_SPEC] + [VMEM_SPEC] * len(args) + [HBM_SPEC] * (len(ahead) + 1),
        out_specs=[VMEM_SPEC] * (own + len(ahead) + len(ks)),
        scratch_shapes=[VM((rows, width), bf16), pltpu.SemaphoreType.DMA((max(1, len(ahead)),)), pltpu.SemaphoreType.DMA((max(1, len(ks)),))],
        compiler_params=pltpu.CompilerParams(vmem_limit_bytes=4 * MIB),
        cost_estimate=cost(4 * width * hidden, 4 * rows * width * hidden),
        name="experts_last" if last is not None else "experts",
    )(place, *args, *[hbm(m) for m, _ in ahead], hbm(down))
    return res[:own], res[own : own + len(ahead)], res[own + len(ahead) :]


def back_kernel(n, place_ref, h_ref, *refs):
    adds, ready, outs = refs[:n], refs[n : 2 * n], refs[2 * n : 4 * n]
    half = outs[0].shape[0]
    for i in range(n):
        value = jnp.dot(h_ref[...], ready[i][...], preferred_element_type=f32) + adds[i][...].astype(f32)
        value = value.astype(bf16)
        outs[2 * i][...] = value[:half]
        outs[2 * i + 1][...] = value[half:]


def back(place, h, adds, ready):
    rows = h.shape[0]
    n, width = len(ready), ready[0].shape[1]
    res = pl.pallas_call(
        functools.partial(back_kernel, n),
        out_shape=[jax.ShapeDtypeStruct((rows // 2, width), bf16) for _ in range(2 * n)],
        in_specs=[SMEM_SPEC] + [VMEM_SPEC] * (1 + 2 * n),
        out_specs=[VMEM_SPEC] * (2 * n),
        compiler_params=pltpu.CompilerParams(vmem_limit_bytes=4 * MIB),
        name="back",
    )(place, h, *adds, *ready)
    return [res[2 * i : 2 * i + 2] for i in range(n)]


def own_kernel(place_ref, h_ref, add_ref, token_ref, wd, a_ref, b_ref, buf, sem):
    loads = col_loads(place_ref, wd, [0], [buf], sem)
    all_of(loads, "start")
    all_of(loads, "wait")
    half = a_ref.shape[0]
    value = jnp.dot(h_ref[...], buf[...], preferred_element_type=f32) + add_ref[...].astype(f32)
    a_ref[...] = value[:half]
    b_ref[...] = value[half:]


def own_block(place, h, add, token, down, width):
    rows, hidden = h.shape
    return pl.pallas_call(
        own_kernel,
        out_shape=[jax.ShapeDtypeStruct((rows // 2, width), f32)] * 2,
        in_specs=[SMEM_SPEC] + [VMEM_SPEC] * 3 + [HBM_SPEC],
        out_specs=[VMEM_SPEC] * 2,
        scratch_shapes=[VM((hidden, width), bf16), pltpu.SemaphoreType.DMA((1,))],
        compiler_params=pltpu.CompilerParams(vmem_limit_bytes=10 * MIB),
        cost_estimate=cost(2 * width * hidden, 2 * rows * width * hidden),
        name="own_block",
    )(place, h, add, token, hbm(down))


def gather_dp(x):
    n = lax.axis_size("dp")
    far = [swap(x, "dp", k) for k in range(2, n, 2)]
    out = [x, swap(x, "dp", 1)]
    for a in far:
        out += [a, swap(a, "dp", 1)]
    return out


def body(
    query,
    key_value_new,
    key_value_cache,
    cache_len,
    out_proj,
    residual,
    norm_gain,
    routes,
    route_weight,
    w_gate,
    w_up,
    w_down,
):
    n_dp = lax.axis_size("dp")
    n_tp = lax.axis_size("tp")
    j, t = lax.axis_index("dp"), lax.axis_index("tp")
    place = jnp.stack([j, t]).astype(jnp.int32)
    total, width = residual.shape
    share = total // n_tp
    keep, sent = list(range(0, n_tp, 2)), list(range(1, n_tp, 2))
    even, odd = list(range(2, n_dp, 2)), list(range(3, n_dp, 2))

    context, proj_weight = attend(place, query, key_value_new, key_value_cache, cache_len, out_proj)

    ctx = gather_dp(context)

    kept, parted = project(place, ctx, proj_weight, total, keep, sent)
    got = swap(parted, "tp", 1)
    (gate0,), token = fetch(place, parted, [(w_gate, 0)], width)
    sums, passed = add_up(kept, got, token)
    got = [swap(passed, "tp", k) for k in keep[1:]]
    (up0, gate1, up1, gate2), token = fetch(
        place, passed, [(w_up, 0), (w_gate, 1), (w_up, 1), (w_gate, 2)], width
    )
    attended, near = stream(place, sums, got, keep[1:], residual, norm_gain, token, keep)
    weight = request_weights(place, routes.T, route_weight.T, near, n_dp // EXPERTS, keep + sent)

    other = swap(near, "tp", 1)
    far_near = [swap(near, "dp", k) for k in even]
    (up2,), token = fetch(place, near, [(w_up, 2)], width)
    other = passed_on(other, token)
    core_near = swap(near, "dp", 1)
    far_other = [swap(other, "dp", k) for k in even]
    core_other = swap(other, "dp", 1)
    halves = [(near, other), (core_near, core_other)]
    for a, b in zip(far_near, far_other):
        halves += [(a, b), (swap(a, "dp", 1), swap(b, "dp", 1))]
    gates, ups = [gate0, gate1, gate2], [up0, up1, up2]
    odd = odd + [1]
    acc, ready = None, {}
    for i in range(n_dp):
        ahead = [(m, k) for m, at in ((w_gate, 0), (w_up, 1)) for k in range(3, n_dp) if i == at]
        downs = {2: odd, n_dp - 1: even}.get(i, [])
        last = (weight, odd, [ready[k] for k in odd]) if i == n_dp - 1 else None
        acc, late, loaded = grow(
            place, halves[i], gates[i], ups[i], acc, ahead, w_down, downs, w_gate.shape[0], last
        )
        for (m, _), v in zip(ahead, late):
            (gates if m is w_gate else ups).append(v)
        ready.update(zip(downs, loaded))
    out_odd, h = acc[:-1], acc[-1]

    crossed = [swap(o, "dp", 1) for o in out_odd]
    sums = back(place, h, crossed[:-1], [ready[k] for k in even])
    there = [swap(s[1], "dp", k) for s, k in zip(sums, even)]
    here = [swap(s[0], "dp", k) for s, k in zip(sums, even)]
    mix_a, mix_b = own_block(place, h, crossed[-1], sums[0][1], w_down, width)
    for x in there:
        mix_b = mix_b + x.astype(f32)
    got = swap(mix_b.astype(bf16), "tp", 1).astype(f32)
    for x in here:
        mix_a = mix_a + x.astype(f32)
    mix = mix_a + got
    result = mix[:share]
    for i, k in enumerate(keep[1:]):
        result = result + swap(mix[(i + 1) * share : (i + 2) * share].astype(bf16), "tp", k).astype(f32)
    return (attended, result.astype(bf16))


def solution(mesh):
    in_specs = (
        P(("grp", "dp"), "tp"),
        P(("grp", "dp"), "tp"),
        P(("grp", "dp"), None, "tp"),
        P(("grp", "dp")),
        P("tp", "dp"),
        P("grp", "dp"),
        P("dp"),
        P("grp", None),
        P("grp", None),
        P(None, ("dp", "tp")),
        P(None, ("dp", "tp")),
        P(("dp", "tp"), None),
    )
    out_specs = (P(("grp", "tp"), "dp"), P(("grp", "tp"), "dp"))
    return jax.shard_map(body, mesh=mesh, in_specs=in_specs, out_specs=out_specs, check_vma=False)
```

```python
import functools

import jax
import jax.numpy as jnp
from jax import lax
from jax.experimental import pallas as pl
from jax.experimental.pallas import tpu as pltpu
from jax.sharding import PartitionSpec as P

QUERY_HEADS = 48
KEY_VALUE_HEADS = 8
HEAD_SIZE = 128
EXPERTS = 4
EPS = 1e-05
TAIL = 128
MIB = 1 << 20
VM = pltpu.VMEM
f32, bf16 = jnp.float32, jnp.bfloat16
SMEM_SPEC = pl.BlockSpec(memory_space=pltpu.SMEM)
HBM_SPEC = pl.BlockSpec(memory_space=pltpu.HBM)
VMEM_SPEC = pl.BlockSpec(memory_space=VM)


def swap(x, axis, k):
    n = lax.axis_size(axis)
    return lax.ppermute(x, axis, [(i, i ^ k) for i in range(n)])


def hbm(x):
    return pltpu.with_memory_space_constraint(x, pltpu.HBM)


def cost(nbytes, flops=0):
    return pl.CostEstimate(flops=int(flops), bytes_accessed=int(nbytes), transcendentals=0)


def row_loads(place_ref, mats, ks, outs, sem):
    loads = []
    for i, k in enumerate(ks):
        width = outs[i].shape[0]
        rows = pl.ds(pl.multiple_of((place_ref[0] ^ k) * width, 128), width)
        loads.append(pltpu.make_async_copy(mats[i].at[rows, :], outs[i], sem.at[i]))
    return loads


def col_loads(place_ref, mat, ks, outs, sem):
    loads = []
    for i, k in enumerate(ks):
        width = outs[i].shape[1]
        cols = pl.ds(pl.multiple_of((place_ref[0] ^ k) * width, 128), width)
        loads.append(pltpu.make_async_copy(mat.at[:, cols], outs[i], sem.at[i]))
    return loads


def all_of(loads, act):
    for c in loads:
        getattr(c, act)()


def attend_kernel(kv, group, batch, _, len_hbm, q_hbm, new_hbm, cache_hbm, w_hbm, *refs):
    out_ref, w_ref, len_ref, q_ref, new_ref, cache, q_scr, new_scr, sem, w_sem, small_sem = refs
    rows, slots = cache.shape[0], cache.shape[1]
    small = [
        pltpu.make_async_copy(a, b, small_sem.at[i])
        for i, (a, b) in enumerate(((q_hbm, q_ref), (new_hbm, new_ref), (len_hbm, len_ref)))
    ]
    all_of(small, "start")
    parts = [pl.ds(i * batch, batch) for i in range(rows // batch)]
    loads = [pltpu.make_async_copy(cache_hbm.at[p], cache.at[p], sem.at[i]) for i, p in enumerate(parts)]
    all_of(loads, "start")
    after = pltpu.make_async_copy(w_hbm, w_ref, w_sem)
    after.start()
    all_of(small, "wait")
    scale = 1.0 / HEAD_SIZE**0.5
    q_scr[...] = jnp.zeros_like(q_scr)
    for h in range(kv):
        for g in range(group):
            lo = (h * group + g) * HEAD_SIZE
            q_scr[h, :, g, :] = q_ref[:, lo : lo + HEAD_SIZE].astype(f32)
    new_scr[...] = new_ref[...].astype(f32)
    lane = lax.broadcasted_iota(jnp.int32, (HEAD_SIZE, HEAD_SIZE), 1)
    row = lax.broadcasted_iota(jnp.int32, (slots + 16, HEAD_SIZE), 0)

    @pl.loop(0, len(parts))
    def _(i):
        base = pl.multiple_of(i * batch, batch)
        p = pl.ds(base, batch)
        length = jnp.zeros((1, HEAD_SIZE), jnp.int32)
        for b in range(batch):
            length = jnp.where(lane[:1] // 8 == b, len_ref[base + b], length)
        valid = (row < length) | (row == slots)
        new = new_scr[p, :]
        pltpu.make_async_copy(cache_hbm.at[p], cache.at[p], sem.at[i]).wait()
        for h in range(kv):
            lo = 2 * h * HEAD_SIZE
            hi = lo + HEAD_SIZE
            q = q_scr[h, p].reshape(batch * 8, HEAD_SIZE).T.astype(bf16)
            wide = jnp.concatenate([jnp.where(lane // 8 == b, q, jnp.zeros_like(q)) for b in range(batch)], axis=0)
            keys = jnp.concatenate([cache[base + b, :, lo:hi] for b in range(batch)], axis=1)
            fresh = jnp.concatenate([new[b : b + 1, lo:hi] for b in range(batch)], axis=1)
            fresh = jnp.broadcast_to(fresh, (16, batch * HEAD_SIZE)).astype(bf16)
            s = jnp.dot(jnp.concatenate([keys, fresh], axis=0), wide, preferred_element_type=f32)
            s = jnp.where(valid, s * scale, -jnp.inf)
            e = jnp.exp(s - jnp.max(s, axis=0, keepdims=True))
            probs = (e * (1.0 / jnp.sum(e, axis=0, keepdims=True))).T
            for b in range(batch):
                new_v = jnp.broadcast_to(new[b : b + 1, hi : hi + HEAD_SIZE], (16, HEAD_SIZE)).astype(bf16)
                vals = jnp.concatenate([cache[base + b, :, hi : hi + HEAD_SIZE], new_v], axis=0)
                q_scr[h, base + b] = jnp.dot(
                    probs[b * 8 : b * 8 + 8].astype(bf16), vals, preferred_element_type=f32
                )

    for h in range(kv):
        for g in range(group):
            lo = (h * group + g) * HEAD_SIZE
            out_ref[:, lo : lo + HEAD_SIZE] = q_scr[h, :, g, :].astype(bf16)
    after.wait()


def attend(place, query, key_value_new, cache, cache_len, out_proj):
    rows, slots, width = cache.shape
    kv = width // (2 * HEAD_SIZE)
    group = QUERY_HEADS // KEY_VALUE_HEADS
    batch = HEAD_SIZE // 8
    return pl.pallas_call(
        functools.partial(attend_kernel, kv, group, batch),
        out_shape=[jax.ShapeDtypeStruct(query.shape, bf16), VM(out_proj.shape, bf16)],
        in_specs=[SMEM_SPEC] + [HBM_SPEC] * 5,
        out_specs=[VMEM_SPEC] * 2,
        scratch_shapes=[
            pltpu.SMEM(cache_len.shape, jnp.int32),
            VM(query.shape, bf16),
            VM(key_value_new.shape, bf16),
            VM(cache.shape, bf16),
            VM((kv, rows, 8, HEAD_SIZE), f32),
            VM(key_value_new.shape, f32),
            pltpu.SemaphoreType.DMA((rows // batch,)),
            pltpu.SemaphoreType.DMA,
            pltpu.SemaphoreType.DMA((3,)),
        ],
        compiler_params=pltpu.CompilerParams(vmem_limit_bytes=10 * MIB),
        cost_estimate=cost(4 * cache.size, 24 * cache.size),
        name="attention",
    )(place, *[hbm(a) for a in (cache_len, query, key_value_new, cache, out_proj)])


def fetch_kernel(ks, place_ref, token_ref, *refs):
    n = len(ks)
    mats, outs, token_out, sem = refs[:n], refs[n : 2 * n], refs[2 * n], refs[2 * n + 1]
    loads = row_loads(place_ref, mats, ks, outs, sem)
    all_of(loads, "start")
    token_out[...] = token_ref[:8, :128]
    all_of(loads, "wait")


def fetch(place, token, wanted, width):
    ks = [k for _, k in wanted]
    n = len(wanted)
    res = pl.pallas_call(
        functools.partial(fetch_kernel, ks),
        out_shape=[VM((width, m.shape[1]), bf16) for m, _ in wanted] + [jax.ShapeDtypeStruct((8, 128), token.dtype)],
        in_specs=[SMEM_SPEC, VMEM_SPEC] + [HBM_SPEC] * n,
        out_specs=[VMEM_SPEC] * (n + 1),
        scratch_shapes=[pltpu.SemaphoreType.DMA((n,))],
        compiler_params=pltpu.CompilerParams(vmem_limit_bytes=MIB),
        cost_estimate=cost(sum(2 * width * m.shape[1] for m, _ in wanted)),
        name="fetch",
    )(place, token, *[hbm(m) for m, _ in wanted])
    return res[:n], res[n]


def project_kernel(keep, sent, place_ref, *refs):
    n_dp = len(refs) - 5
    ctx, w_ref, keep_ref, send_ref, held, prod = refs[:n_dp], *refs[n_dp:]
    j, t = place_ref[0], place_ref[1]
    rows = ctx[0].shape[0]
    share = keep_ref.shape[0] // len(keep)
    for k in range(n_dp):
        held[pl.ds(pl.multiple_of((j ^ k) * rows, rows), rows), :] = ctx[k][...]
    prod[...] = jnp.dot(held[...], w_ref[...], preferred_element_type=f32)
    for i, k in enumerate(sent):
        block = pl.ds(pl.multiple_of((t ^ k) * share, share), share)
        send_ref[i * share : (i + 1) * share, :] = prod[block, :].astype(bf16)
    for i, k in enumerate(keep):
        block = pl.ds(pl.multiple_of((t ^ k) * share, share), share)
        keep_ref[i * share : (i + 1) * share, :] = prod[block, :]


def project(place, ctx, out_proj, total, keep, sent):
    width = out_proj.shape[1]
    share = total // (len(keep) + len(sent))
    depth = out_proj.shape[0]
    return pl.pallas_call(
        functools.partial(project_kernel, keep, sent),
        out_shape=[
            jax.ShapeDtypeStruct((len(keep) * share, width), f32),
            jax.ShapeDtypeStruct((len(sent) * share, width), bf16),
        ],
        in_specs=[SMEM_SPEC] + [VMEM_SPEC] * (len(ctx) + 1),
        out_specs=[VMEM_SPEC] * 2,
        scratch_shapes=[VM((total, depth), bf16), VM((total, width), f32)],
        compiler_params=pltpu.CompilerParams(vmem_limit_bytes=4 * MIB),
        cost_estimate=cost(2 * out_proj.size, 2 * total * out_proj.size),
        name="projection",
    )(place, *ctx, out_proj)


def sum_kernel(own_ref, got_ref, *refs):
    sum_ref, pass_ref = refs[-2:]
    total = own_ref[...] + got_ref[...].astype(f32)
    sum_ref[...] = total
    pass_ref[...] = total.astype(bf16)


def pass_kernel(x_ref, *refs):
    refs[-1][...] = x_ref[...]


def passed_on(x, *tokens):
    return pl.pallas_call(
        pass_kernel,
        out_shape=jax.ShapeDtypeStruct(x.shape, x.dtype),
        in_specs=[VMEM_SPEC] * (1 + len(tokens)),
        out_specs=VMEM_SPEC,
        compiler_params=pltpu.CompilerParams(vmem_limit_bytes=2 * MIB),
        name="passed_on",
    )(x, *tokens)


def add_up(own, got, *tokens):
    return pl.pallas_call(
        sum_kernel,
        out_shape=[jax.ShapeDtypeStruct(own.shape, f32), jax.ShapeDtypeStruct(own.shape, bf16)],
        in_specs=[VMEM_SPEC] * (2 + len(tokens)),
        out_specs=[VMEM_SPEC] * 2,
        compiler_params=pltpu.CompilerParams(vmem_limit_bytes=4 * MIB),
        name="pair_sum",
    )(own, got, *tokens)


def stream_kernel(keep, arrived, place_ref, sum_ref, *refs):
    n = len(arrived)
    got, (res_ref, gain_ref, _, att_ref, msg_ref) = refs[:n], refs[n:]
    share, width = att_ref.shape
    t = place_ref[1]
    for i, k in enumerate(keep):
        x = sum_ref[i * share : (i + 1) * share, :]
        for a, m in enumerate(arrived):
            place = keep.index(k ^ m)
            x = x + got[a][place * share : (place + 1) * share, :].astype(f32)
        x = x + res_ref[pl.ds(pl.multiple_of((t ^ k) * share, share), share), :].astype(f32)
        if i == 0:
            att_ref[...] = x.astype(bf16)
        rows = slice(i * share, (i + 1) * share)
        msg_ref[rows, :width] = (x * gain_ref[...][None, :]).astype(bf16)
        left = jnp.sum(x * x, axis=1, keepdims=True)
        lane = lax.broadcasted_iota(jnp.int32, (share, TAIL), 1)
        tail = jnp.zeros((share, TAIL), f32)
        for piece in range(3):
            high = left.astype(bf16).astype(f32)
            tail = jnp.where(lane == piece, high, tail)
            left = left - high
        msg_ref[rows, width:] = tail.astype(bf16)


def stream(place, total, got, arrived, residual, gain, token, keep):
    rows, width = total.shape
    share = rows // len(keep)
    return pl.pallas_call(
        functools.partial(stream_kernel, keep, arrived),
        out_shape=[VM((share, width), bf16), jax.ShapeDtypeStruct((rows, width + TAIL), bf16)],
        in_specs=[SMEM_SPEC] + [VMEM_SPEC] * (len(got) + 4),
        out_specs=[VMEM_SPEC] * 2,
        compiler_params=pltpu.CompilerParams(vmem_limit_bytes=4 * MIB),
        name="residual_stream",
    )(place, total, *got, residual, gain, token)


def weights_kernel(owners, order, place_ref, routes_ref, given_ref, token_ref, out_ref):
    j, t = place_ref[0], place_ref[1]
    total = out_ref.shape[0]
    share = total // len(order)
    mine = jnp.where(routes_ref[...] == j // owners, given_ref[...], 0.0)
    mine = jnp.sum(mine, axis=0, keepdims=True)
    lane = lax.broadcasted_iota(jnp.int32, (share, total), 1)
    row = lax.broadcasted_iota(jnp.int32, (share, total), 0)
    for i, k in enumerate(order):
        picked = jnp.where(lane == (t ^ k) * share + row, mine, 0.0)
        out_ref[i * share : (i + 1) * share, :] = jnp.sum(picked, axis=1, keepdims=True)


def request_weights(place, routes, given, token, owners, order):
    return pl.pallas_call(
        functools.partial(weights_kernel, owners, order),
        out_shape=jax.ShapeDtypeStruct((routes.shape[1], 1), f32),
        in_specs=[SMEM_SPEC] + [VMEM_SPEC] * 3,
        out_specs=VMEM_SPEC,
        compiler_params=pltpu.CompilerParams(vmem_limit_bytes=4 * MIB),
        name="request_weights",
    )(place, routes, given, token)


def join(x_ref, parts, width):
    at = 0
    sq = []
    for p in parts:
        n = p.shape[0]
        x_ref[at : at + n, :] = p[:, :width]
        sq.append(jnp.sum(p[:, width:].astype(f32), axis=1, keepdims=True))
        at += n
    return jnp.concatenate(sq, axis=0)


def products(x_refs, gates, ups, cols):
    g = sum(jnp.dot(x[...], w[:, cols], preferred_element_type=f32) for x, w in zip(x_refs, gates))
    u = sum(jnp.dot(x[...], w[:, cols], preferred_element_type=f32) for x, w in zip(x_refs, ups))
    return g, u


def halves_of(hidden, work):
    @pl.loop(0, 2)
    def _(c):
        work(pl.ds(pl.multiple_of(c * (hidden // 2), 128), hidden // 2))


def grow_kernel(first, row_ks, ks, place_ref, *refs):
    r, m = len(row_ks), len(ks)
    (a_ref, b_ref, gate, up), refs = refs[:4], refs[4:]
    if not first:
        (in_g, in_u, in_sq), refs = refs[:3], refs[3:]
    mats, wd, (acc_g, acc_u, sq_ref), refs = refs[:r], refs[r], refs[r + 1 : r + 4], refs[r + 4 :]
    row_loaded, loaded, (x_ref, row_sem, sem) = refs[:r], refs[r : r + m], refs[r + m :]
    loads = row_loads(place_ref, mats, row_ks, row_loaded, row_sem) + col_loads(place_ref, wd, ks, loaded, sem)
    all_of(loads, "start")
    sq = join(x_ref, (a_ref, b_ref), x_ref.shape[1])
    sq_ref[...] = sq if first else sq + in_sq[...]

    def work(cols):
        g, u = products([x_ref], [gate], [up], cols)
        acc_g[:, cols] = g if first else g + in_g[:, cols]
        acc_u[:, cols] = u if first else u + in_u[:, cols]

    halves_of(acc_g.shape[1], work)
    all_of(loads, "wait")


def grow(place, parts, gate, up, acc, ahead, down, ks):
    rows = parts[0].shape[0] + parts[1].shape[0]
    width, hidden = gate.shape
    r, m = len(ahead), len(ks)
    args = [*parts, gate, up] + (list(acc) if acc is not None else [])
    res = pl.pallas_call(
        functools.partial(grow_kernel, acc is None, [k for _, k in ahead], ks),
        out_shape=[jax.ShapeDtypeStruct((rows, c), f32) for c in (hidden, hidden, 1)]
        + [VM((width, hidden), bf16) for _ in ahead]
        + [VM((hidden, width), bf16) for _ in ks],
        in_specs=[SMEM_SPEC] + [VMEM_SPEC] * len(args) + [HBM_SPEC] * (r + 1),
        out_specs=[VMEM_SPEC] * (3 + r + m),
        scratch_shapes=[
            VM((rows, width), bf16),
            pltpu.SemaphoreType.DMA((max(1, r),)),
            pltpu.SemaphoreType.DMA((max(1, m),)),
        ],
        compiler_params=pltpu.CompilerParams(vmem_limit_bytes=4 * MIB),
        cost_estimate=cost(4 * width * hidden, 4 * rows * width * hidden),
        name="experts",
    )(place, *args, *[hbm(m) for m, _ in ahead], hbm(down))
    return res[:3], res[3 : 3 + r], res[3 + r :]


def last_kernel(n, a, late, even, model, place_ref, *refs):
    parts, gates, ups, refs = refs[: 2 * n], refs[2 * n : 3 * n], refs[3 * n : 4 * n], refs[4 * n :]
    (in_g, in_u, in_sq, weight), downs, wd, refs = refs[:4], refs[4 : 3 + a], refs[3 + a], refs[4 + a :]
    b = len(even)
    outs, h_ref, loaded, (x_ref, down, sem, late_sem) = refs[:a], refs[a], refs[a + 1 : a + 1 + b], refs[a + 1 + b :]
    late_load = col_loads(place_ref, wd, [late], [down], late_sem)
    loads = col_loads(place_ref, wd, even, loaded, sem)
    all_of(late_load + loads, "start")
    xs = [x_ref.at[i] for i in range(n)]
    sq = in_sq[...] + sum(join(xs[i], parts[2 * i : 2 * i + 2], x_ref.shape[2]) for i in range(n))
    scale = lax.rsqrt(sq / model + EPS)
    up_scale = scale * weight[...]

    def work(cols):
        g, u = products(xs, gates, ups, cols)
        g = (g + in_g[:, cols]) * scale
        u = (u + in_u[:, cols]) * up_scale
        h_ref[:, cols] = (g / (1.0 + jnp.exp(-g)) * u).astype(bf16)

    halves_of(h_ref.shape[1], work)
    for i, w in enumerate([*downs, down]):
        if w is down:
            all_of(late_load, "wait")
        outs[i][...] = jnp.dot(h_ref[...], w[...], preferred_element_type=f32).astype(bf16)
    all_of(loads, "wait")


def last_blocks(place, parts, gates, ups, acc, weight, downs, down, late, even):
    n, a = len(gates), len(downs) + 1
    rows = parts[0].shape[0] + parts[1].shape[0]
    width, hidden = gates[0].shape
    res = pl.pallas_call(
        functools.partial(last_kernel, n, a, late, even, down.shape[1]),
        out_shape=[jax.ShapeDtypeStruct((rows, width), bf16) for _ in range(a)]
        + [jax.ShapeDtypeStruct((rows, hidden), bf16)]
        + [VM((hidden, width), bf16) for _ in even],
        in_specs=[SMEM_SPEC] + [VMEM_SPEC] * (4 * n + 3 + a) + [HBM_SPEC],
        out_specs=[VMEM_SPEC] * (a + 1 + len(even)),
        scratch_shapes=[
            VM((n, rows, width), bf16),
            VM((hidden, width), bf16),
            pltpu.SemaphoreType.DMA((len(even),)),
            pltpu.SemaphoreType.DMA((1,)),
        ],
        compiler_params=pltpu.CompilerParams(vmem_limit_bytes=10 * MIB),
        cost_estimate=cost(4 * n * width * hidden, 4 * n * rows * width * hidden),
        name="experts_last",
    )(place, *parts, *gates, *ups, *acc, weight, *downs, hbm(down))
    return res[:a], res[a], res[a + 1 :]


def back_kernel(n, place_ref, h_ref, *refs):
    adds, ready, outs = refs[:n], refs[n : 2 * n], refs[2 * n : 4 * n]
    half = outs[0].shape[0]
    for i in range(n):
        value = jnp.dot(h_ref[...], ready[i][...], preferred_element_type=f32) + adds[i][...].astype(f32)
        value = value.astype(bf16)
        outs[2 * i][...] = value[:half]
        outs[2 * i + 1][...] = value[half:]


def back(place, h, adds, ready):
    rows = h.shape[0]
    n, width = len(ready), ready[0].shape[1]
    res = pl.pallas_call(
        functools.partial(back_kernel, n),
        out_shape=[jax.ShapeDtypeStruct((rows // 2, width), bf16) for _ in range(2 * n)],
        in_specs=[SMEM_SPEC] + [VMEM_SPEC] * (1 + 2 * n),
        out_specs=[VMEM_SPEC] * (2 * n),
        compiler_params=pltpu.CompilerParams(vmem_limit_bytes=4 * MIB),
        name="back",
    )(place, h, *adds, *ready)
    return [res[2 * i : 2 * i + 2] for i in range(n)]


def own_kernel(place_ref, h_ref, add_ref, token_ref, wd, a_ref, b_ref, buf, sem):
    loads = col_loads(place_ref, wd, [0], [buf], sem)
    all_of(loads, "start")
    all_of(loads, "wait")
    half = a_ref.shape[0]
    value = jnp.dot(h_ref[...], buf[...], preferred_element_type=f32) + add_ref[...].astype(f32)
    a_ref[...] = value[:half]
    b_ref[...] = value[half:]


def own_block(place, h, add, token, down, width):
    rows, hidden = h.shape
    return pl.pallas_call(
        own_kernel,
        out_shape=[jax.ShapeDtypeStruct((rows // 2, width), f32)] * 2,
        in_specs=[SMEM_SPEC] + [VMEM_SPEC] * 3 + [HBM_SPEC],
        out_specs=[VMEM_SPEC] * 2,
        scratch_shapes=[VM((hidden, width), bf16), pltpu.SemaphoreType.DMA((1,))],
        compiler_params=pltpu.CompilerParams(vmem_limit_bytes=10 * MIB),
        cost_estimate=cost(2 * width * hidden, 2 * rows * width * hidden),
        name="own_block",
    )(place, h, add, token, hbm(down))


def gather_dp(x):
    n = lax.axis_size("dp")
    far = [swap(x, "dp", k) for k in range(2, n, 2)]
    out = [x, swap(x, "dp", 1)]
    for a in far:
        out += [a, swap(a, "dp", 1)]
    return out


def body(
    query,
    key_value_new,
    key_value_cache,
    cache_len,
    out_proj,
    residual,
    norm_gain,
    routes,
    route_weight,
    w_gate,
    w_up,
    w_down,
):
    n_dp = lax.axis_size("dp")
    n_tp = lax.axis_size("tp")
    j, t = lax.axis_index("dp"), lax.axis_index("tp")
    place = jnp.stack([j, t]).astype(jnp.int32)
    total, width = residual.shape
    share = total // n_tp
    keep, sent = list(range(0, n_tp, 2)), list(range(1, n_tp, 2))
    even, odd = list(range(2, n_dp, 2)), list(range(3, n_dp, 2))

    context, proj_weight = attend(place, query, key_value_new, key_value_cache, cache_len, out_proj)

    ctx = gather_dp(context)

    kept, parted = project(place, ctx, proj_weight, total, keep, sent)
    got = swap(parted, "tp", 1)
    (gate0,), token = fetch(place, parted, [(w_gate, 0)], width)
    weight = request_weights(place, routes.T, route_weight.T, token, n_dp // EXPERTS, keep + sent)
    sums, passed = add_up(kept, got, token, weight)
    got = [swap(passed, "tp", k) for k in keep[1:]]
    (up0, gate1, up1, *gates), token = fetch(
        place, passed, [(w_up, 0), (w_gate, 1), (w_up, 1)] + [(w_gate, k) for k in even], width
    )
    attended, near = stream(place, sums, got, keep[1:], residual, norm_gain, token, keep)

    other = swap(near, "tp", 1)
    far_near = [swap(near, "dp", k) for k in even]
    ups, token = fetch(place, near, [(w_up, k) for k in even], width)
    other = passed_on(other, token)
    core_near = swap(near, "dp", 1)
    far_other = [swap(other, "dp", k) for k in even]
    core_other = swap(other, "dp", 1)
    acc, odd_gates, _ = grow(place, (passed_on(near, *far_near), other), gate0, up0, None, [(w_gate, k) for k in odd], w_down, [])
    acc, odd_ups, _ = grow(place, (core_near, core_other), gate1, up1, acc, [(w_up, k) for k in odd], w_down, [])
    far_other = [passed_on(x, acc[2]) for x in far_other]
    last, downs = [], []
    for i, (a, b) in enumerate(zip(far_near, far_other)):
        last += [swap(a, "dp", 1), swap(b, "dp", 1)]
        acc, _, loaded = grow(place, (a, b), gates[i], ups[i], acc, [], w_down, odd if i == 0 else [])
        downs += loaded
    out_odd, h, ready = last_blocks(place, last, odd_gates, odd_ups, acc, weight, downs, w_down, 1, even)

    crossed = [swap(o, "dp", 1) for o in out_odd]
    sums = back(place, h, crossed[:-1], ready)
    there = [swap(s[1], "dp", k) for s, k in zip(sums, even)]
    here = [swap(s[0], "dp", k) for s, k in zip(sums, even)]
    mix_a, mix_b = own_block(place, h, crossed[-1], sums[0][1], w_down, width)
    for x in there:
        mix_b = mix_b + x.astype(f32)
    got = swap(mix_b.astype(bf16), "tp", 1).astype(f32)
    for x in here:
        mix_a = mix_a + x.astype(f32)
    mix = mix_a + got
    result = mix[:share]
    for i, k in enumerate(keep[1:]):
        result = result + swap(mix[(i + 1) * share : (i + 2) * share].astype(bf16), "tp", k).astype(f32)
    return (attended, result.astype(bf16))


def solution(mesh):
    in_specs = (
        P(("grp", "dp"), "tp"),
        P(("grp", "dp"), "tp"),
        P(("grp", "dp"), None, "tp"),
        P(("grp", "dp")),
        P("tp", "dp"),
        P("grp", "dp"),
        P("dp"),
        P("grp", None),
        P("grp", None),
        P(None, ("dp", "tp")),
        P(None, ("dp", "tp")),
        P(("dp", "tp"), None),
    )
    out_specs = (P(("grp", "tp"), "dp"), P(("grp", "tp"), "dp"))
    return jax.shard_map(body, mesh=mesh, in_specs=in_specs, out_specs=out_specs, check_vma=False)
```

```python
import functools

import jax
import jax.numpy as jnp
from jax import lax
from jax.experimental import pallas as pl
from jax.experimental.pallas import tpu as pltpu
from jax.sharding import PartitionSpec as P

QUERY_HEADS = 48
KEY_VALUE_HEADS = 8
HEAD_SIZE = 128
EXPERTS = 4
EPS = 1e-05
TAIL = 128
MIB = 1 << 20
VM = pltpu.VMEM
f32, bf16 = jnp.float32, jnp.bfloat16
SMEM_SPEC = pl.BlockSpec(memory_space=pltpu.SMEM)
HBM_SPEC = pl.BlockSpec(memory_space=pltpu.HBM)
VMEM_SPEC = pl.BlockSpec(memory_space=VM)


def swap(x, axis, k):
    n = lax.axis_size(axis)
    return lax.ppermute(x, axis, [(i, i ^ k) for i in range(n)])


def hbm(x):
    return pltpu.with_memory_space_constraint(x, pltpu.HBM)


def cost(nbytes, flops=0):
    return pl.CostEstimate(flops=int(flops), bytes_accessed=int(nbytes), transcendentals=0)


def row_loads(place_ref, mats, ks, outs, sem):
    loads = []
    for i, k in enumerate(ks):
        width = outs[i].shape[0]
        rows = pl.ds(pl.multiple_of((place_ref[0] ^ k) * width, 128), width)
        loads.append(pltpu.make_async_copy(mats[i].at[rows, :], outs[i], sem.at[i]))
    return loads


def col_loads(place_ref, mat, ks, outs, sem):
    loads = []
    for i, k in enumerate(ks):
        width = outs[i].shape[1]
        cols = pl.ds(pl.multiple_of((place_ref[0] ^ k) * width, 128), width)
        loads.append(pltpu.make_async_copy(mat.at[:, cols], outs[i], sem.at[i]))
    return loads


def all_of(loads, act):
    for c in loads:
        getattr(c, act)()


def attend_kernel(kv, group, batch, _, len_hbm, q_hbm, new_hbm, cache_hbm, w_hbm, *refs):
    out_ref, w_ref, len_ref, q_ref, new_ref, cache, q_scr, new_scr, sem, w_sem, small_sem = refs
    rows, slots = cache.shape[0], cache.shape[1]
    small = [
        pltpu.make_async_copy(a, b, small_sem.at[i])
        for i, (a, b) in enumerate(((q_hbm, q_ref), (new_hbm, new_ref), (len_hbm, len_ref)))
    ]
    all_of(small, "start")
    parts = [pl.ds(i * batch, batch) for i in range(rows // batch)]
    loads = [pltpu.make_async_copy(cache_hbm.at[p], cache.at[p], sem.at[i]) for i, p in enumerate(parts)]
    all_of(loads, "start")
    after = pltpu.make_async_copy(w_hbm, w_ref, w_sem)
    after.start()
    all_of(small, "wait")
    scale = 1.0 / HEAD_SIZE**0.5
    q_scr[...] = jnp.zeros_like(q_scr)
    for h in range(kv):
        for g in range(group):
            lo = (h * group + g) * HEAD_SIZE
            q_scr[h, :, g, :] = q_ref[:, lo : lo + HEAD_SIZE].astype(f32)
    new_scr[...] = new_ref[...].astype(f32)
    lane = lax.broadcasted_iota(jnp.int32, (HEAD_SIZE, HEAD_SIZE), 1)
    row = lax.broadcasted_iota(jnp.int32, (slots + 16, HEAD_SIZE), 0)

    @pl.loop(0, len(parts))
    def _(i):
        base = pl.multiple_of(i * batch, batch)
        p = pl.ds(base, batch)
        length = jnp.zeros((1, HEAD_SIZE), jnp.int32)
        for b in range(batch):
            length = jnp.where(lane[:1] // 8 == b, len_ref[base + b], length)
        valid = (row < length) | (row == slots)
        new = new_scr[p, :]
        pltpu.make_async_copy(cache_hbm.at[p], cache.at[p], sem.at[i]).wait()
        for h in range(kv):
            lo = 2 * h * HEAD_SIZE
            hi = lo + HEAD_SIZE
            q = q_scr[h, p].reshape(batch * 8, HEAD_SIZE).T.astype(bf16)
            wide = jnp.concatenate([jnp.where(lane // 8 == b, q, jnp.zeros_like(q)) for b in range(batch)], axis=0)
            keys = jnp.concatenate([cache[base + b, :, lo:hi] for b in range(batch)], axis=1)
            fresh = jnp.concatenate([new[b : b + 1, lo:hi] for b in range(batch)], axis=1)
            fresh = jnp.broadcast_to(fresh, (16, batch * HEAD_SIZE)).astype(bf16)
            s = jnp.dot(jnp.concatenate([keys, fresh], axis=0), wide, preferred_element_type=f32)
            s = jnp.where(valid, s * scale, -jnp.inf)
            e = jnp.exp(s - jnp.max(s, axis=0, keepdims=True))
            probs = (e * (1.0 / jnp.sum(e, axis=0, keepdims=True))).T
            for b in range(batch):
                new_v = jnp.broadcast_to(new[b : b + 1, hi : hi + HEAD_SIZE], (16, HEAD_SIZE)).astype(bf16)
                vals = jnp.concatenate([cache[base + b, :, hi : hi + HEAD_SIZE], new_v], axis=0)
                q_scr[h, base + b] = jnp.dot(
                    probs[b * 8 : b * 8 + 8].astype(bf16), vals, preferred_element_type=f32
                )

    for h in range(kv):
        for g in range(group):
            lo = (h * group + g) * HEAD_SIZE
            out_ref[:, lo : lo + HEAD_SIZE] = q_scr[h, :, g, :].astype(bf16)
    after.wait()


def attend(place, query, key_value_new, cache, cache_len, out_proj):
    rows, slots, width = cache.shape
    kv = width // (2 * HEAD_SIZE)
    group = QUERY_HEADS // KEY_VALUE_HEADS
    batch = HEAD_SIZE // 8
    return pl.pallas_call(
        functools.partial(attend_kernel, kv, group, batch),
        out_shape=[jax.ShapeDtypeStruct(query.shape, bf16), VM(out_proj.shape, bf16)],
        in_specs=[SMEM_SPEC] + [HBM_SPEC] * 5,
        out_specs=[VMEM_SPEC] * 2,
        scratch_shapes=[
            pltpu.SMEM(cache_len.shape, jnp.int32),
            VM(query.shape, bf16),
            VM(key_value_new.shape, bf16),
            VM(cache.shape, bf16),
            VM((kv, rows, 8, HEAD_SIZE), f32),
            VM(key_value_new.shape, f32),
            pltpu.SemaphoreType.DMA((rows // batch,)),
            pltpu.SemaphoreType.DMA,
            pltpu.SemaphoreType.DMA((3,)),
        ],
        compiler_params=pltpu.CompilerParams(vmem_limit_bytes=10 * MIB),
        cost_estimate=cost(4 * cache.size, 24 * cache.size),
        name="attention",
    )(place, *[hbm(a) for a in (cache_len, query, key_value_new, cache, out_proj)])


def fetch_kernel(ks, place_ref, token_ref, *refs):
    n = len(ks)
    mats, outs, token_out, sem = refs[:n], refs[n : 2 * n], refs[2 * n], refs[2 * n + 1]
    loads = row_loads(place_ref, mats, ks, outs, sem)
    all_of(loads, "start")
    token_out[...] = token_ref[:8, :128]
    all_of(loads, "wait")


def fetch(place, token, wanted, width):
    ks = [k for _, k in wanted]
    n = len(wanted)
    res = pl.pallas_call(
        functools.partial(fetch_kernel, ks),
        out_shape=[VM((width, m.shape[1]), bf16) for m, _ in wanted] + [jax.ShapeDtypeStruct((8, 128), token.dtype)],
        in_specs=[SMEM_SPEC, VMEM_SPEC] + [HBM_SPEC] * n,
        out_specs=[VMEM_SPEC] * (n + 1),
        scratch_shapes=[pltpu.SemaphoreType.DMA((n,))],
        compiler_params=pltpu.CompilerParams(vmem_limit_bytes=MIB),
        cost_estimate=cost(sum(2 * width * m.shape[1] for m, _ in wanted)),
        name="fetch",
    )(place, token, *[hbm(m) for m, _ in wanted])
    return res[:n], res[n]


def project_kernel(keep, sent, place_ref, *refs):
    n_dp = len(refs) - 5
    ctx, w_ref, keep_ref, send_ref, held, prod = refs[:n_dp], *refs[n_dp:]
    j, t = place_ref[0], place_ref[1]
    rows = ctx[0].shape[0]
    share = keep_ref.shape[0] // len(keep)
    for k in range(n_dp):
        held[pl.ds(pl.multiple_of((j ^ k) * rows, rows), rows), :] = ctx[k][...]
    prod[...] = jnp.dot(held[...], w_ref[...], preferred_element_type=f32)
    for i, k in enumerate(sent):
        block = pl.ds(pl.multiple_of((t ^ k) * share, share), share)
        send_ref[i * share : (i + 1) * share, :] = prod[block, :].astype(bf16)
    for i, k in enumerate(keep):
        block = pl.ds(pl.multiple_of((t ^ k) * share, share), share)
        keep_ref[i * share : (i + 1) * share, :] = prod[block, :]


def project(place, ctx, out_proj, total, keep, sent):
    width = out_proj.shape[1]
    share = total // (len(keep) + len(sent))
    depth = out_proj.shape[0]
    return pl.pallas_call(
        functools.partial(project_kernel, keep, sent),
        out_shape=[
            jax.ShapeDtypeStruct((len(keep) * share, width), f32),
            jax.ShapeDtypeStruct((len(sent) * share, width), bf16),
        ],
        in_specs=[SMEM_SPEC] + [VMEM_SPEC] * (len(ctx) + 1),
        out_specs=[VMEM_SPEC] * 2,
        scratch_shapes=[VM((total, depth), bf16), VM((total, width), f32)],
        compiler_params=pltpu.CompilerParams(vmem_limit_bytes=4 * MIB),
        cost_estimate=cost(2 * out_proj.size, 2 * total * out_proj.size),
        name="projection",
    )(place, *ctx, out_proj)


def sum_kernel(own_ref, got_ref, *refs):
    sum_ref, pass_ref = refs[-2:]
    total = own_ref[...] + got_ref[...].astype(f32)
    sum_ref[...] = total
    pass_ref[...] = total.astype(bf16)


def pass_kernel(x_ref, *refs):
    refs[-1][...] = x_ref[...]


def passed_on(x, *tokens):
    return pl.pallas_call(
        pass_kernel,
        out_shape=jax.ShapeDtypeStruct(x.shape, x.dtype),
        in_specs=[VMEM_SPEC] * (1 + len(tokens)),
        out_specs=VMEM_SPEC,
        compiler_params=pltpu.CompilerParams(vmem_limit_bytes=2 * MIB),
        name="passed_on",
    )(x, *tokens)


def add_up(own, got, *tokens):
    return pl.pallas_call(
        sum_kernel,
        out_shape=[jax.ShapeDtypeStruct(own.shape, f32), jax.ShapeDtypeStruct(own.shape, bf16)],
        in_specs=[VMEM_SPEC] * (2 + len(tokens)),
        out_specs=[VMEM_SPEC] * 2,
        compiler_params=pltpu.CompilerParams(vmem_limit_bytes=4 * MIB),
        name="pair_sum",
    )(own, got, *tokens)


def stream_kernel(keep, arrived, place_ref, sum_ref, *refs):
    n = len(arrived)
    got, (res_ref, gain_ref, _, att_ref, msg_ref) = refs[:n], refs[n:]
    share, width = att_ref.shape
    t = place_ref[1]
    for i, k in enumerate(keep):
        x = sum_ref[i * share : (i + 1) * share, :]
        for a, m in enumerate(arrived):
            place = keep.index(k ^ m)
            x = x + got[a][place * share : (place + 1) * share, :].astype(f32)
        x = x + res_ref[pl.ds(pl.multiple_of((t ^ k) * share, share), share), :].astype(f32)
        if i == 0:
            att_ref[...] = x.astype(bf16)
        rows = slice(i * share, (i + 1) * share)
        msg_ref[rows, :width] = (x * gain_ref[...][None, :]).astype(bf16)
        left = jnp.sum(x * x, axis=1, keepdims=True)
        lane = lax.broadcasted_iota(jnp.int32, (share, TAIL), 1)
        tail = jnp.zeros((share, TAIL), f32)
        for piece in range(3):
            high = left.astype(bf16).astype(f32)
            tail = jnp.where(lane == piece, high, tail)
            left = left - high
        msg_ref[rows, width:] = tail.astype(bf16)


def stream(place, total, got, arrived, residual, gain, token, keep):
    rows, width = total.shape
    share = rows // len(keep)
    return pl.pallas_call(
        functools.partial(stream_kernel, keep, arrived),
        out_shape=[VM((share, width), bf16), jax.ShapeDtypeStruct((rows, width + TAIL), bf16)],
        in_specs=[SMEM_SPEC] + [VMEM_SPEC] * (len(got) + 4),
        out_specs=[VMEM_SPEC] * 2,
        compiler_params=pltpu.CompilerParams(vmem_limit_bytes=4 * MIB),
        name="residual_stream",
    )(place, total, *got, residual, gain, token)


def weights_kernel(owners, order, place_ref, routes_ref, given_ref, token_ref, out_ref):
    j, t = place_ref[0], place_ref[1]
    total = out_ref.shape[0]
    share = total // len(order)
    mine = jnp.where(routes_ref[...] == j // owners, given_ref[...], 0.0)
    mine = jnp.sum(mine, axis=0, keepdims=True)
    lane = lax.broadcasted_iota(jnp.int32, (share, total), 1)
    row = lax.broadcasted_iota(jnp.int32, (share, total), 0)
    for i, k in enumerate(order):
        picked = jnp.where(lane == (t ^ k) * share + row, mine, 0.0)
        out_ref[i * share : (i + 1) * share, :] = jnp.sum(picked, axis=1, keepdims=True)


def request_weights(place, routes, given, token, owners, order):
    return pl.pallas_call(
        functools.partial(weights_kernel, owners, order),
        out_shape=jax.ShapeDtypeStruct((routes.shape[1], 1), f32),
        in_specs=[SMEM_SPEC] + [VMEM_SPEC] * 3,
        out_specs=VMEM_SPEC,
        compiler_params=pltpu.CompilerParams(vmem_limit_bytes=4 * MIB),
        name="request_weights",
    )(place, routes, given, token)


def join(x_ref, parts, width):
    at = 0
    sq = []
    for p in parts:
        n = p.shape[0]
        x_ref[at : at + n, :] = p[:, :width]
        sq.append(jnp.sum(p[:, width:].astype(f32), axis=1, keepdims=True))
        at += n
    return jnp.concatenate(sq, axis=0)


def products(x_refs, gates, ups, cols):
    g = sum(jnp.dot(x[...], w[:, cols], preferred_element_type=f32) for x, w in zip(x_refs, gates))
    u = sum(jnp.dot(x[...], w[:, cols], preferred_element_type=f32) for x, w in zip(x_refs, ups))
    return g, u


def halves_of(hidden, work):
    @pl.loop(0, 2)
    def _(c):
        work(pl.ds(pl.multiple_of(c * (hidden // 2), 128), hidden // 2))


def grow_kernel(first, row_ks, ks, place_ref, *refs):
    r, m = len(row_ks), len(ks)
    (a_ref, b_ref, gate, up), refs = refs[:4], refs[4:]
    if not first:
        (in_g, in_u, in_sq), refs = refs[:3], refs[3:]
    mats, wd, (acc_g, acc_u, sq_ref), refs = refs[:r], refs[r], refs[r + 1 : r + 4], refs[r + 4 :]
    row_loaded, loaded, (x_ref, row_sem, sem) = refs[:r], refs[r : r + m], refs[r + m :]
    loads = row_loads(place_ref, mats, row_ks, row_loaded, row_sem) + col_loads(place_ref, wd, ks, loaded, sem)
    all_of(loads, "start")
    sq = join(x_ref, (a_ref, b_ref), x_ref.shape[1])
    sq_ref[...] = sq if first else sq + in_sq[...]

    def work(cols):
        g, u = products([x_ref], [gate], [up], cols)
        acc_g[:, cols] = g if first else g + in_g[:, cols]
        acc_u[:, cols] = u if first else u + in_u[:, cols]

    halves_of(acc_g.shape[1], work)
    all_of(loads, "wait")


def grow(place, parts, gate, up, acc, ahead, down, ks):
    rows = parts[0].shape[0] + parts[1].shape[0]
    width, hidden = gate.shape
    r, m = len(ahead), len(ks)
    args = [*parts, gate, up] + (list(acc) if acc is not None else [])
    res = pl.pallas_call(
        functools.partial(grow_kernel, acc is None, [k for _, k in ahead], ks),
        out_shape=[jax.ShapeDtypeStruct((rows, c), f32) for c in (hidden, hidden, 1)]
        + [VM((width, hidden), bf16) for _ in ahead]
        + [VM((hidden, width), bf16) for _ in ks],
        in_specs=[SMEM_SPEC] + [VMEM_SPEC] * len(args) + [HBM_SPEC] * (r + 1),
        out_specs=[VMEM_SPEC] * (3 + r + m),
        scratch_shapes=[
            VM((rows, width), bf16),
            pltpu.SemaphoreType.DMA((max(1, r),)),
            pltpu.SemaphoreType.DMA((max(1, m),)),
        ],
        compiler_params=pltpu.CompilerParams(vmem_limit_bytes=4 * MIB),
        cost_estimate=cost(4 * width * hidden, 4 * rows * width * hidden),
        name="experts",
    )(place, *args, *[hbm(m) for m, _ in ahead], hbm(down))
    return res[:3], res[3 : 3 + r], res[3 + r :]


def last_kernel(n, a, late, even, model, place_ref, *refs):
    parts, gates, ups, refs = refs[: 2 * n], refs[2 * n : 3 * n], refs[3 * n : 4 * n], refs[4 * n :]
    (in_g, in_u, in_sq, weight), downs, wd, refs = refs[:4], refs[4 : 3 + a], refs[3 + a], refs[4 + a :]
    b = len(even)
    outs, h_ref, loaded, (x_ref, down, sem, late_sem) = refs[:a], refs[a], refs[a + 1 : a + 1 + b], refs[a + 1 + b :]
    late_load = col_loads(place_ref, wd, [late], [down], late_sem)
    loads = col_loads(place_ref, wd, even, loaded, sem)
    all_of(late_load + loads, "start")
    xs = [x_ref.at[i] for i in range(n)]
    sq = in_sq[...] + sum(join(xs[i], parts[2 * i : 2 * i + 2], x_ref.shape[2]) for i in range(n))
    scale = lax.rsqrt(sq / model + EPS)
    up_scale = scale * weight[...]

    def work(cols):
        g, u = products(xs, gates, ups, cols)
        g = (g + in_g[:, cols]) * scale
        u = (u + in_u[:, cols]) * up_scale
        h_ref[:, cols] = (g / (1.0 + jnp.exp(-g)) * u).astype(bf16)

    halves_of(h_ref.shape[1], work)
    for i, w in enumerate([*downs, down]):
        if w is down:
            all_of(late_load, "wait")
        outs[i][...] = jnp.dot(h_ref[...], w[...], preferred_element_type=f32).astype(bf16)
    all_of(loads, "wait")


def last_blocks(place, parts, gates, ups, acc, weight, downs, down, late, even):
    n, a = len(gates), len(downs) + 1
    rows = parts[0].shape[0] + parts[1].shape[0]
    width, hidden = gates[0].shape
    res = pl.pallas_call(
        functools.partial(last_kernel, n, a, late, even, down.shape[1]),
        out_shape=[jax.ShapeDtypeStruct((rows, width), bf16) for _ in range(a)]
        + [jax.ShapeDtypeStruct((rows, hidden), bf16)]
        + [VM((hidden, width), bf16) for _ in even],
        in_specs=[SMEM_SPEC] + [VMEM_SPEC] * (4 * n + 3 + a) + [HBM_SPEC],
        out_specs=[VMEM_SPEC] * (a + 1 + len(even)),
        scratch_shapes=[
            VM((n, rows, width), bf16),
            VM((hidden, width), bf16),
            pltpu.SemaphoreType.DMA((len(even),)),
            pltpu.SemaphoreType.DMA((1,)),
        ],
        compiler_params=pltpu.CompilerParams(vmem_limit_bytes=10 * MIB),
        cost_estimate=cost(4 * n * width * hidden, 4 * n * rows * width * hidden),
        name="experts_last",
    )(place, *parts, *gates, *ups, *acc, weight, *downs, hbm(down))
    return res[:a], res[a], res[a + 1 :]


def down_kernel(n, h_ref, *refs):
    for w, out in zip(refs[:n], refs[n:]):
        out[...] = jnp.dot(h_ref[...], w[...], preferred_element_type=f32).astype(out.dtype)


def down_blocks(h, downs, types):
    n, rows, (hidden, width) = len(downs), h.shape[0], downs[0].shape
    return pl.pallas_call(
        functools.partial(down_kernel, n),
        out_shape=[jax.ShapeDtypeStruct((rows, width), t) for t in types],
        in_specs=[VMEM_SPEC] * (1 + n),
        out_specs=[VMEM_SPEC] * n,
        compiler_params=pltpu.CompilerParams(vmem_limit_bytes=4 * MIB),
        cost_estimate=cost(2 * n * width * hidden, 2 * n * rows * width * hidden),
        name="down",
    )(h, *downs)


def back_kernel(n, *refs):
    own, adds, outs = refs[:n], refs[n : 2 * n], refs[2 * n :]
    half = outs[0].shape[0]
    for i in range(n):
        for part in range(2):
            rows = slice(part * half, (part + 1) * half)
            outs[2 * i + part][...] = (own[i][rows, :] + adds[i][rows, :].astype(f32)).astype(bf16)


def back(own, adds):
    n, (rows, width) = len(own), own[0].shape
    res = pl.pallas_call(
        functools.partial(back_kernel, n),
        out_shape=[jax.ShapeDtypeStruct((rows // 2, width), bf16) for _ in range(2 * n)],
        in_specs=[VMEM_SPEC] * (2 * n),
        out_specs=[VMEM_SPEC] * (2 * n),
        compiler_params=pltpu.CompilerParams(vmem_limit_bytes=4 * MIB),
        name="back",
    )(*own, *adds)
    return [res[2 * i : 2 * i + 2] for i in range(n)]


def own_kernel(place_ref, h_ref, add_ref, token_ref, wd, a_ref, b_ref, buf, sem):
    loads = col_loads(place_ref, wd, [0], [buf], sem)
    all_of(loads, "start")
    all_of(loads, "wait")
    half = a_ref.shape[0]
    value = jnp.dot(h_ref[...], buf[...], preferred_element_type=f32) + add_ref[...].astype(f32)
    a_ref[...] = value[:half]
    b_ref[...] = value[half:]


def own_block(place, h, add, token, down, width):
    rows, hidden = h.shape
    return pl.pallas_call(
        own_kernel,
        out_shape=[jax.ShapeDtypeStruct((rows // 2, width), f32)] * 2,
        in_specs=[SMEM_SPEC] + [VMEM_SPEC] * 3 + [HBM_SPEC],
        out_specs=[VMEM_SPEC] * 2,
        scratch_shapes=[VM((hidden, width), bf16), pltpu.SemaphoreType.DMA((1,))],
        compiler_params=pltpu.CompilerParams(vmem_limit_bytes=10 * MIB),
        cost_estimate=cost(2 * width * hidden, 2 * rows * width * hidden),
        name="own_block",
    )(place, h, add, token, hbm(down))


def gather_dp(x):
    n = lax.axis_size("dp")
    far = [swap(x, "dp", k) for k in range(2, n, 2)]
    out = [x, swap(x, "dp", 1)]
    for a in far:
        out += [a, swap(a, "dp", 1)]
    return out


def body(
    query,
    key_value_new,
    key_value_cache,
    cache_len,
    out_proj,
    residual,
    norm_gain,
    routes,
    route_weight,
    w_gate,
    w_up,
    w_down,
):
    n_dp = lax.axis_size("dp")
    n_tp = lax.axis_size("tp")
    j, t = lax.axis_index("dp"), lax.axis_index("tp")
    place = jnp.stack([j, t]).astype(jnp.int32)
    total, width = residual.shape
    share = total // n_tp
    keep, sent = list(range(0, n_tp, 2)), list(range(1, n_tp, 2))
    even, odd = list(range(2, n_dp, 2)), list(range(3, n_dp, 2))

    context, proj_weight = attend(place, query, key_value_new, key_value_cache, cache_len, out_proj)

    ctx = gather_dp(context)

    kept, parted = project(place, ctx, proj_weight, total, keep, sent)
    got = swap(parted, "tp", 1)
    (gate0,), token = fetch(place, parted, [(w_gate, 0)], width)
    weight = request_weights(place, routes.T, route_weight.T, token, n_dp // EXPERTS, keep + sent)
    sums, passed = add_up(kept, got, token, weight)
    got = [swap(passed, "tp", k) for k in keep[1:]]
    (up0, gate1, up1, *gates), token = fetch(
        place, passed, [(w_up, 0), (w_gate, 1), (w_up, 1)] + [(w_gate, k) for k in even], width
    )
    attended, near = stream(place, sums, got, keep[1:], residual, norm_gain, token, keep)

    other = swap(near, "tp", 1)
    far_near = [swap(near, "dp", k) for k in even]
    ups, token = fetch(place, near, [(w_up, k) for k in even], width)
    other = passed_on(other, token)
    core_near = swap(near, "dp", 1)
    far_other = [swap(other, "dp", k) for k in even]
    core_other = swap(other, "dp", 1)
    acc, odd_gates, _ = grow(place, (passed_on(near, *far_near), other), gate0, up0, None, [(w_gate, k) for k in odd], w_down, [])
    acc, odd_ups, _ = grow(place, (core_near, core_other), gate1, up1, acc, [(w_up, k) for k in odd], w_down, [])
    far_other = [passed_on(x, acc[2]) for x in far_other]
    last, downs = [], []
    for i, (a, b) in enumerate(zip(far_near, far_other)):
        last += [swap(a, "dp", 1), swap(b, "dp", 1)]
        acc, _, loaded = grow(place, (a, b), gates[i], ups[i], acc, [], w_down, odd if i == 0 else [])
        downs += loaded
    out_odd, h, ready = last_blocks(place, last, odd_gates, odd_ups, acc, weight, downs, w_down, 1, even)

    crossed = [swap(o, "dp", 1) for o in out_odd]
    sums = back(down_blocks(h, ready, [f32] * len(even)), crossed[:-1])
    there = [swap(s[1], "dp", k) for s, k in zip(sums, even)]
    here = [swap(s[0], "dp", k) for s, k in zip(sums, even)]
    mix_a, mix_b = own_block(place, h, crossed[-1], sums[0][1], w_down, width)
    for x in there:
        mix_b = mix_b + x.astype(f32)
    got = swap(mix_b.astype(bf16), "tp", 1).astype(f32)
    for x in here:
        mix_a = mix_a + x.astype(f32)
    mix = mix_a + got
    result = mix[:share]
    for i, k in enumerate(keep[1:]):
        result = result + swap(mix[(i + 1) * share : (i + 2) * share].astype(bf16), "tp", k).astype(f32)
    return (attended, result.astype(bf16))


def solution(mesh):
    in_specs = (
        P(("grp", "dp"), "tp"),
        P(("grp", "dp"), "tp"),
        P(("grp", "dp"), None, "tp"),
        P(("grp", "dp")),
        P("tp", "dp"),
        P("grp", "dp"),
        P("dp"),
        P("grp", None),
        P("grp", None),
        P(None, ("dp", "tp")),
        P(None, ("dp", "tp")),
        P(("dp", "tp"), None),
    )
    out_specs = (P(("grp", "tp"), "dp"), P(("grp", "tp"), "dp"))
    return jax.shard_map(body, mesh=mesh, in_specs=in_specs, out_specs=out_specs, check_vma=False)
```
